256 devices in a mesh: section: 4 (over x), expert: 32 (over z, y), dp: 2 (over core).
Axes of the slice: x: 4, y: 4, z: 8, core: 2. Of those that a mesh axis runs over, the one named last changes fastest.
Arguments:
- tokens: bfloat16 [2048, 4096], P(('expert', 'dp')), may hold values from -6 to 6
- routing: int32 [2048, 8], P(('expert', 'dp')), may hold values from 0 to 63, all different within a row; in each aligned block of 32 rows (0 to 31, 32 to 63, ...) at most 8 rows name the same one
- gate_weights: float32 [2048, 8], P(('expert', 'dp')), may hold values from 0.05 to 0.3
- w_gate: bfloat16 [64, 4096, 1536], P(('expert', 'dp'), None, 'section'), may hold values from -0.09375 to 0.09375
- w_up: bfloat16 [64, 4096, 1536], P(('expert', 'dp'), None, 'section'), may hold values from -0.09375 to 0.09375
- w_down: bfloat16 [64, 1536, 4096], P(('expert', 'dp'), 'section'), may hold values from -0.15625 to 0.15625
Outputs:
- combined: bfloat16 [2048, 4096], P(('expert', 'dp'), 'section')
The draws below stay inside these ranges and needn't reach their ends.
Inputs may be any that keep to these rules, and one draw needn't show every extreme that they name: `routing`: each row names 8 different experts. In each aligned block of 32 rows (the rows of one device) no expert is named by more than 8 rows, and in some block an expert is named by exactly 8 rows.
All inputs are finite; a program needn't handle non-finite values.
Results may differ from the reference program's by a relative error of at most 0.011.
Values may be sent and summed in bfloat16 or wider, within the bound.
No kernel may reach another device: no remote copies, remote signals or barrier semaphores. Data moves between devices by JAX's collectives and lax.ppermute only.
A program may use at most 128 MiB of HBM per device.

```python
import math
import jax
import jax.numpy as jnp
import numpy as np
from jax import lax

D = 4096
FF = 1536
TOP = 8
TOK_DEV = 32
EXPERTS = 64
TOKENS = 2048
CAP = 8


def steps_of(rng, extent, split, smallest, top_value):
    loudness, own = 1.0, jax.random.fold_in(rng, 6)
    for dim, parts in split:
        heights = jnp.exp(jax.random.uniform(jax.random.fold_in(own, dim), (parts,), jnp.float32, smallest / len(split), top_value / len(split)))
        loudness = loudness * jnp.repeat(heights, extent[dim] // parts).reshape([-1 if axis == dim else 1 for axis in range(len(extent))])
    return loudness


def assign_block(own_key, own, number, rows, amount, top, reach, skew):
    sequence = jax.random.permutation(own_key, amount)
    packed, usual = shares(amount, rows * top, reach, skew, True), shares(amount, rows * top, reach, skew, False)
    places = jnp.arange(amount)

    def named(sizes, turn):
        used = int((sizes > 0).sum())
        fixed = max(1, used // 4)
        moved = fixed + (places - fixed + turn * (used - fixed)) % max(1, amount - fixed)
        return jnp.zeros((amount,), jnp.int32).at[sequence[jnp.where(places < fixed, places, moved)]].set(jnp.asarray(sizes, jnp.int32))

    sizes = jnp.where(number % 4 == 0, named(packed, number // 4), named(usual, number - number // 4 - 1))
    mixed = jax.random.permutation(jax.random.fold_in(own, 3), amount)
    donor, receiver = mixed[0:amount // 2 * 2:2], mixed[1:amount // 2 * 2:2]
    margin = jnp.minimum(sizes[donor] - 1, reach - sizes[receiver]) // 2
    margin = jnp.where((donor == sequence[0]) | (receiver == sequence[0]) | (sizes[receiver] == 0), 0, jnp.maximum(margin, 0))
    moved = jax.random.randint(jax.random.fold_in(own, 4), (amount // 2,), 0, 1 << 20) % (margin + 1)
    sizes = sizes.at[donor].add(-moved).at[receiver].add(moved)
    labels = jnp.searchsorted(jnp.cumsum(sizes), jnp.arange(rows * top), side="right").astype(jnp.int32)
    table = labels.reshape(top, rows).T
    table = table[jax.random.permutation(jax.random.fold_in(own, 1), rows)]
    turn = jax.random.randint(jax.random.fold_in(own, 2), (rows, 1), 0, top)
    return jnp.take_along_axis(table, (jnp.arange(top)[None, :] + turn) % top, axis=1)


def shares(amount, total, most, slope, full):
    portions = [(1 << 20) // math.isqrt(standing ** slope) + 1 for standing in range(1, amount + 1)]
    largest = most if full else min(most, max(-(-total // amount), total * portions[0] // sum(portions)))
    least = 1 if total - largest >= amount - 1 else 0
    holding, rest = [largest] + [least] * (amount - 1), total - largest - least * (amount - 1)
    while rest > 0:
        free = [i for i in range(1, amount) if holding[i] < largest] or [i for i in range(1, amount) if holding[i] < most]
        pool, left = sum([portions[i] for i in free]), rest
        for i in free:
            more = min(most - holding[i], max(1, left * portions[i] // pool), rest)
            holding[i] = holding[i] + more
            rest = rest - more
    return np.array(holding)


def scatter_about(key, dims, scale, limit, shards=(), kind=jnp.bfloat16):
    result = jax.random.normal(key, dims, jnp.float32) * scale
    if len(shards) > 0:
        result = steps_of(key, dims, shards, -0.22, 0.18) * result
    return jnp.clip(result, min=-limit, max=limit).astype(kind)


def setup_inputs(seed: int = 0) -> dict:
    arg_keys = jax.random.split(jax.random.key(seed), 7)
    tokens = scatter_about(arg_keys[0], (TOKENS, D), 1.0, 6.0, ((0, 64),))
    routing_keys = jax.random.split(jax.random.fold_in(arg_keys[1], 1), TOKENS // TOK_DEV)
    routing_turns = jax.random.permutation(jax.random.fold_in(arg_keys[1], 3), TOKENS // TOK_DEV)
    routing = jax.vmap(lambda own, number: assign_block(jax.random.fold_in(arg_keys[1], 2), own, number, TOK_DEV, EXPERTS, TOP, CAP, 2))(routing_keys, routing_turns).reshape((TOKENS, TOP))
    gate_weights = jnp.clip(0.05 + 0.25 * jax.random.uniform(arg_keys[2], (TOKENS, TOP), jnp.float32) ** steps_of(arg_keys[2], (TOKENS, TOP), ((0, 64),), -0.2, 0.2), 0.05, 0.3)
    w_gate = scatter_about(arg_keys[3], (EXPERTS, D, FF), D ** -0.5, 0.09375, ((0, 64), (2, 4)))
    w_up = scatter_about(arg_keys[4], (EXPERTS, D, FF), D ** -0.5, 0.09375, ((0, 64), (2, 4)))
    w_down = scatter_about(arg_keys[5], (EXPERTS, FF, D), FF ** -0.5, 0.15625, ((0, 64), (1, 4)))
    return dict(tokens=tokens, routing=routing, gate_weights=gate_weights, w_gate=w_gate, w_up=w_up, w_down=w_down)


def reference(tokens, routing, gate_weights, w_gate, w_up, w_down):
    token_count = tokens.shape[0]
    blocks = token_count // TOK_DEV
    one_hot = (routing[:, :, None] == jnp.arange(EXPERTS, dtype=jnp.int32)[None, None, :]).astype(jnp.int32)
    grouped = one_hot.reshape(blocks, TOK_DEV * TOP, EXPERTS)
    earlier = jnp.cumsum(grouped, axis=1) - grouped
    slot_rank = jnp.sum(earlier * grouped, axis=2).reshape(token_count, TOP)
    source = (jnp.arange(token_count, dtype=jnp.int32) // TOK_DEV)[:, None]
    position = source * CAP + slot_rank
    slot_count = blocks * CAP
    owners = jnp.broadcast_to(jnp.arange(token_count, dtype=jnp.int32)[:, None], (token_count, TOP))
    slot_table = jnp.full((EXPERTS, slot_count), token_count, jnp.int32).at[routing, position].set(owners)
    gate_table = jnp.zeros((EXPERTS, slot_count), jnp.float32).at[routing, position].set(gate_weights)
    padded = jnp.concatenate([tokens, jnp.zeros((1, tokens.shape[1]), tokens.dtype)], axis=0)

    def accumulate(running, expert_id):
        picked_rows = padded[slot_table[expert_id]]
        gate_proj = jnp.dot(picked_rows, w_gate[expert_id], preferred_element_type=jnp.float32)
        up_proj = jnp.dot(picked_rows, w_up[expert_id], preferred_element_type=jnp.float32)
        hidden = (jax.nn.silu(gate_proj) * up_proj).astype(jnp.bfloat16)
        expert_out = jnp.dot(hidden, w_down[expert_id], preferred_element_type=jnp.float32)
        running = running.at[slot_table[expert_id]].add(gate_table[expert_id][:, None] * expert_out)
        return running, None

    start_total = jnp.zeros((token_count + 1, tokens.shape[1]), jnp.float32)
    running, unused = lax.scan(accumulate, start_total, jnp.arange(EXPERTS, dtype=jnp.int32))
    return running[:token_count].astype(jnp.bfloat16)
```

```python
import jax
import jax.numpy as jnp
from jax import lax
from jax.sharding import PartitionSpec as P

ED = ("expert", "dp")
BF = jnp.bfloat16
F32 = jnp.float32


def dot(a, b):
    return jnp.dot(a, b, preferred_element_type=F32)


def on_device(tokens, routing, gate_weights, w_gate, w_up, w_down):
    toks, width = tokens.shape
    fanout = routing.shape[1]
    experts = lax.axis_size(ED)
    sections = lax.axis_size("section")
    cap = min(toks, max(2, 2 * toks * fanout // experts))
    quarter = width // sections
    s = lax.axis_index("section")
    right = [(k, (k + 1) % sections) for k in range(sections)]
    left = [(k, (k - 1) % sections) for k in range(sections)]

    def to_right(v):
        return lax.ppermute(v, "section", right)

    def to_left(v):
        return lax.ppermute(v, "section", left)

    match = routing[:, :, None] == jnp.arange(experts, dtype=jnp.int32)[None, None, :]
    named = jnp.any(match, axis=1)
    weight = jnp.sum(jnp.where(match, gate_weights[:, :, None], 0.0), axis=1)
    counts = named.astype(jnp.int32)
    rank = jnp.cumsum(counts, axis=0) - counts
    place = named[:, :, None] & (rank[:, :, None] == jnp.arange(cap, dtype=jnp.int32)[None, None, :])
    pick = place.astype(BF).reshape(toks, experts * cap)
    spread = jnp.where(place, weight[:, :, None], 0.0).reshape(toks, experts * cap)
    spread_hi = spread.astype(BF)
    spread_lo = (spread - spread_hi.astype(F32)).astype(BF)
    spread2 = jnp.concatenate([spread_hi, spread_lo], axis=0)

    own_cols = lax.dynamic_slice_in_dim(tokens, s * quarter, quarter, axis=1)
    outgoing = lax.dot_general(
        pick, own_cols, (((0,), (0,)), ((), ())), preferred_element_type=F32
    ).astype(BF)
    received = lax.all_to_all(
        outgoing.reshape(experts, cap, quarter), ED, split_axis=0, concat_axis=0, tiled=True
    ).reshape(experts * cap, quarter)
    rows = experts * cap
    half = rows // 2

    def k_part(block, q):
        q = q % sections
        g = lax.dynamic_slice_in_dim(w_gate[0], q * quarter, quarter, axis=0)
        u = lax.dynamic_slice_in_dim(w_up[0], q * quarter, quarter, axis=0)
        return dot(block, g), dot(block, u)

    a, b = received[:half], received[half:]
    r_a = to_right(a)
    l_b = to_left(b)
    r_b = to_right(b)
    l_a = to_left(a)
    rr_a = to_right(r_a)
    ll_b = to_left(l_b)
    from_left = jnp.concatenate([r_a, r_b], axis=0)
    from_right = jnp.concatenate([l_a, l_b], axis=0)
    across = jnp.concatenate([rr_a, ll_b], axis=0)
    gate, up = k_part(received, s)
    for block, q in ((from_left, s + 3), (from_right, s + 1), (across, s + 2)):
        g, u = k_part(block, q)
        gate, up = gate + g, up + u
    hidden = (jax.nn.silu(gate) * up).astype(BF)

    def down(h, q):
        q = q % sections
        return dot(h, lax.dynamic_slice_in_dim(w_down[0], q * quarter, quarter, axis=1))

    h_a, h_b = hidden[:half], hidden[half:]
    far_a = to_right(down(h_a, s + 2).astype(BF))
    far_b = to_left(down(h_b, s + 2).astype(BF))
    near_b = to_right(down(h_b, s + 1).astype(BF))
    near_a = to_left(down(h_a, s + 3).astype(BF))
    relay_a = to_right((down(h_a, s + 1) + far_a.astype(F32)).astype(BF))
    relay_b = to_left((down(h_b, s + 3) + far_b.astype(F32)).astype(BF))
    own_a = down(h_a, s) + near_a.astype(F32) + relay_a.astype(F32)
    own_b = down(h_b, s) + near_b.astype(F32) + relay_b.astype(F32)
    summed = jnp.concatenate([own_a, own_b], axis=0).astype(BF)
    returned = lax.all_to_all(
        summed.reshape(experts, cap, quarter), ED, split_axis=0, concat_axis=0, tiled=True
    ).reshape(rows, quarter)
    both = dot(spread2, returned)
    return (both[:toks] + both[toks:]).astype(BF)


def solution(mesh):
    placed = (
        P(ED, None),
        P(ED, None),
        P(ED, None),
        P(ED, None, "section"),
        P(ED, None, "section"),
        P(ED, "section", None),
    )
    return jax.shard_map(
        on_device,
        mesh=mesh,
        in_specs=placed,
        out_specs=P(ED, "section"),
        check_vma=False,
    )
```

```python
import jax
import jax.numpy as jnp
from jax import lax
from jax.sharding import PartitionSpec as P

ED = ("expert", "dp")
BF = jnp.bfloat16
F32 = jnp.float32
CHUNKS = 2


def dot(a, b):
    return jnp.dot(a, b, preferred_element_type=F32)


def on_device(tokens, routing, gate_weights, w_gate, w_up, w_down):
    toks, width = tokens.shape
    fanout = routing.shape[1]
    experts = lax.axis_size(ED)
    sections = lax.axis_size("section")
    cap = min(toks, max(2, 2 * toks * fanout // experts))
    quarter = width // sections
    s = lax.axis_index("section")
    right = [(k, (k + 1) % sections) for k in range(sections)]
    left = [(k, (k - 1) % sections) for k in range(sections)]

    def to_right(v):
        return lax.ppermute(v, "section", right)

    def to_left(v):
        return lax.ppermute(v, "section", left)

    match = routing[:, :, None] == jnp.arange(experts, dtype=jnp.int32)[None, None, :]
    named = jnp.any(match, axis=1)
    weight = jnp.sum(jnp.where(match, gate_weights[:, :, None], 0.0), axis=1)
    counts = named.astype(jnp.int32)
    rank = jnp.cumsum(counts, axis=0) - counts
    place = named[:, :, None] & (rank[:, :, None] == jnp.arange(cap, dtype=jnp.int32)[None, None, :])
    pick = place.astype(BF).reshape(toks, experts * cap)
    spread = jnp.where(place, weight[:, :, None], 0.0).reshape(toks, experts * cap)
    spread_hi = spread.astype(BF)
    spread_lo = (spread - spread_hi.astype(F32)).astype(BF)
    spread2 = jnp.concatenate([spread_hi, spread_lo], axis=0)

    rows = experts * cap
    half = rows // 2
    part = quarter // CHUNKS

    def exchange(v):
        return lax.all_to_all(
            v.reshape(experts, cap, part), ED, split_axis=0, concat_axis=0, tiled=True
        ).reshape(rows, part)

    def span(q, c):
        return (q % sections) * quarter + c * part

    received = []
    for c in range(CHUNKS):
        cols = lax.dynamic_slice_in_dim(tokens, span(s, c), part, axis=1)
        outgoing = lax.dot_general(
            pick, cols, (((0,), (0,)), ((), ())), preferred_element_type=F32
        ).astype(BF)
        received.append(exchange(outgoing))

    def k_part(block, q, c):
        g = lax.dynamic_slice_in_dim(w_gate[0], span(q, c), part, axis=0)
        u = lax.dynamic_slice_in_dim(w_up[0], span(q, c), part, axis=0)
        return dot(block, g), dot(block, u)

    gate = up = jnp.zeros((), F32)
    for c in range(CHUNKS):
        block = received[c]
        from_left = to_right(block)
        from_right = to_left(block)
        across = jnp.concatenate([to_right(from_left[:half]), to_left(from_right[half:])], axis=0)
        for piece, q in ((block, s), (from_left, s + 3), (from_right, s + 1), (across, s + 2)):
            g, u = k_part(piece, q, c)
            gate, up = gate + g, up + u
    hidden = (jax.nn.silu(gate) * up).astype(BF)

    def down(h, q, c):
        return dot(h, lax.dynamic_slice_in_dim(w_down[0], span(q, c), part, axis=1))

    h_a, h_b = hidden[:half], hidden[half:]
    returned = []
    for c in range(CHUNKS):
        got_l = to_right(
            jnp.concatenate([down(h_a, s + 2, c), down(h_b, s + 1, c)], axis=0).astype(BF)
        )
        got_r = to_left(
            jnp.concatenate([down(h_a, s + 3, c), down(h_b, s + 2, c)], axis=0).astype(BF)
        )
        relay_a = to_right((down(h_a, s + 1, c) + got_l[:half].astype(F32)).astype(BF))
        relay_b = to_left((down(h_b, s + 3, c) + got_r[half:].astype(F32)).astype(BF))
        near = jnp.concatenate([got_r[:half], got_l[half:]], axis=0).astype(F32)
        relayed = jnp.concatenate([relay_a, relay_b], axis=0).astype(F32)
        returned.append(exchange((down(hidden, s, c) + near + relayed).astype(BF)))
    both = dot(spread2, jnp.concatenate(returned, axis=1))
    return (both[:toks] + both[toks:]).astype(BF)


def solution(mesh):
    placed = (
        P(ED, None),
        P(ED, None),
        P(ED, None),
        P(ED, None, "section"),
        P(ED, None, "section"),
        P(ED, "section", None),
    )
    return jax.shard_map(
        on_device,
        mesh=mesh,
        in_specs=placed,
        out_specs=P(ED, "section"),
        check_vma=False,
    )
```

```python
import jax
import jax.numpy as jnp
from jax import lax
from jax.experimental import pallas as pl
from jax.experimental.pallas import tpu as pltpu
from jax.sharding import PartitionSpec as P

ED = ("expert", "dp")
BF = jnp.bfloat16
F32 = jnp.float32
OUT_WIDTHS = (640, 384)
BACK_WIDTHS = (384, 640)
VMEM = pl.BlockSpec(memory_space=pltpu.VMEM)
SMEM = pl.BlockSpec(memory_space=pltpu.SMEM)
ANY = pl.BlockSpec(memory_space=pl.ANY)
PARAMS = pltpu.CompilerParams(vmem_limit_bytes=40 * 1024 * 1024)


def dot(a, b):
    return jnp.dot(a, b, preferred_element_type=F32)


def cost(flops, read):
    return pl.CostEstimate(flops=flops, bytes_accessed=read, transcendentals=0)


def tie(value, *others):
    return lax.optimization_barrier((value,) + others)[0]


def make_slots(section, tokens, routing, gate_weights, cap, experts, widths):
    toks, fanout = routing.shape
    slots = experts * cap
    quarter = sum(widths)

    def kernel(s_ref, routing_ref, weights_ref, tokens_ref, *outs):
        slot = lax.broadcasted_iota(jnp.int32, (toks, slots), 1)
        expert, order = lax.div(slot, cap), lax.rem(slot, cap)
        named = jnp.zeros((toks, slots), F32)
        weight = jnp.zeros((toks, slots), F32)
        for k in range(fanout):
            hit = routing_ref[:, k : k + 1] == expert
            named = jnp.where(hit, 1.0, named)
            weight = jnp.where(hit, weights_ref[:, k : k + 1], weight)
        before = (
            lax.broadcasted_iota(jnp.int32, (toks, toks), 0)
            > lax.broadcasted_iota(jnp.int32, (toks, toks), 1)
        )
        earlier = dot(jnp.where(before, 1.0, 0.0).astype(BF), named.astype(BF))
        place = jnp.where(earlier == order.astype(F32), named, 0.0)
        rows = lax.dot_general(
            place.astype(BF),
            tokens_ref[...],
            (((0,), (0,)), ((), ())),
            preferred_element_type=F32,
        ).astype(BF)
        start = 0
        for out, width in zip(outs, widths):
            out[...] = rows[:, start : start + width]
            start += width
        spread = place * weight
        high = spread.astype(BF)
        outs[-1][...] = jnp.concatenate([high, (spread - high.astype(F32)).astype(BF)], axis=0)

    return pl.pallas_call(
        kernel,
        grid_spec=pltpu.PrefetchScalarGridSpec(
            num_scalar_prefetch=1,
            grid=(1,),
            in_specs=[
                pl.BlockSpec((toks, fanout), lambda i, s: (0, 0)),
                pl.BlockSpec((toks, fanout), lambda i, s: (0, 0)),
                pl.BlockSpec((toks, quarter), lambda i, s: (0, s[0])),
            ],
            out_specs=[pl.BlockSpec((slots, w), lambda i, s: (0, 0)) for w in widths]
            + [pl.BlockSpec((2 * toks, slots), lambda i, s: (0, 0))],
        ),
        out_shape=[jax.ShapeDtypeStruct((slots, w), BF) for w in widths]
        + [jax.ShapeDtypeStruct((2 * toks, slots), BF)],
        compiler_params=PARAMS,
        cost_estimate=cost(2 * slots * toks * quarter, 2 * slots * quarter),
        name="slots",
    )(section, routing, gate_weights, tokens)


def gate_up(offsets, blocks, w_gate, w_up, total=None, down=None):
    rows = blocks[0].shape[0]
    widths = [b.shape[1] for b in blocks]
    hid = w_gate.shape[2]
    n = len(blocks)
    has_total = total is not None
    if down is not None:
        w_down, down_offsets, down_widths = down
        m = len(down_widths)

    def kernel(*refs):
        refs = list(refs)
        off_ref = refs.pop(0)
        down_off_ref = refs.pop(0) if down is not None else None
        block_refs = [refs.pop(0) for _ in range(n)]
        total_ref = refs.pop(0) if has_total else None
        g_ref, u_ref = refs.pop(0), refs.pop(0)
        d_ref = refs.pop(0) if down is not None else None
        outs = [refs.pop(0) for _ in range(1 if down is None else 1 + m)]
        wbuf, sem = refs.pop(0), refs.pop(0)
        copies = []
        start = 0
        for i, width in enumerate(widths):
            at = pl.ds(pl.multiple_of(off_ref[i], 128), width)
            pair = (
                pltpu.make_async_copy(
                    g_ref.at[0, at, :], wbuf.at[pl.ds(start, width), pl.ds(0, hid)], sem.at[2 * i]
                ),
                pltpu.make_async_copy(
                    u_ref.at[0, at, :],
                    wbuf.at[pl.ds(start, width), pl.ds(hid, hid)],
                    sem.at[2 * i + 1],
                ),
            )
            for c in pair:
                c.start()
            copies.append((pair, start, width))
            start += width
        downs = []
        if down is not None:
            dbuf, dsem = refs.pop(0), refs.pop(0)
            place = 0
            for i, width in enumerate(down_widths):
                c = pltpu.make_async_copy(
                    d_ref.at[0, :, pl.ds(pl.multiple_of(down_off_ref[i], 128), width)],
                    dbuf.at[:, pl.ds(place, width)],
                    dsem.at[i],
                )
                c.start()
                downs.append(c)
                place += width
        acc = total_ref[...] if has_total else None
        for (pair, start, width), block_ref in zip(copies, block_refs):
            for c in pair:
                c.wait()
            term = dot(block_ref[...], wbuf[start : start + width, :])
            acc = term if acc is None else acc + term
        if down is None:
            outs[0][...] = acc
            return
        gate, up = acc[:, :hid], acc[:, hid:]
        hidden = (gate / (1.0 + jnp.exp(-gate)) * up).astype(BF)
        outs[0][...] = hidden
        place = 0
        for c, width, out in zip(downs, down_widths, outs[1:]):
            c.wait()
            out[...] = dot(hidden, dbuf[:, place : place + width]).astype(BF)
            place += width

    scratch = [pltpu.VMEM((sum(widths), 2 * hid), BF), pltpu.SemaphoreType.DMA((2 * n,))]
    ins = [offsets] + ([down_offsets] if down is not None else []) + list(blocks)
    specs = [SMEM] * (1 if down is None else 2) + [VMEM] * n
    if has_total:
        ins.append(total)
        specs.append(VMEM)
    ins += [w_gate, w_up]
    specs += [ANY, ANY]
    flops = 2 * rows * sum(widths) * 2 * hid
    read = 2 * sum(widths) * (2 * hid + rows) + 4 * rows * 2 * hid
    if down is None:
        shapes = [jax.ShapeDtypeStruct((rows, 2 * hid), F32)]
    else:
        ins.append(w_down)
        specs.append(ANY)
        shapes = [jax.ShapeDtypeStruct((rows, hid), BF)]
        shapes += [jax.ShapeDtypeStruct((rows, w), BF) for w in down_widths]
        scratch += [pltpu.VMEM((hid, sum(down_widths)), BF), pltpu.SemaphoreType.DMA((m,))]
        flops += 2 * rows * hid * sum(down_widths)
        read += 2 * sum(down_widths) * (rows + hid)
    out = pl.pallas_call(
        kernel,
        in_specs=specs,
        out_specs=[VMEM] * len(shapes),
        out_shape=shapes,
        scratch_shapes=scratch,
        compiler_params=PARAMS,
        cost_estimate=cost(flops, read),
        name="gate_up" if down is None else "gate_up_down",
    )(*ins)
    return out[0] if down is None else out


def project(offsets, widths, hidden, w_down, addends=()):
    rows, hid = hidden.shape
    n = len(widths)
    k = len(addends)

    def kernel(off_ref, h_ref, d_ref, *refs):
        adds, outs, (dbuf, sem) = refs[:k], refs[k : k + n], refs[k + n :]
        copies = []
        place = 0
        for i, width in enumerate(widths):
            c = pltpu.make_async_copy(
                d_ref.at[0, :, pl.ds(pl.multiple_of(off_ref[i], 128), width)],
                dbuf.at[:, pl.ds(place, width)],
                sem.at[i],
            )
            c.start()
            copies.append((c, place, width))
            place += width
        for (c, place, width), out in zip(copies, outs):
            c.wait()
            value = dot(h_ref[...], dbuf[:, place : place + width])
            for a in adds:
                value = value + a[...].astype(F32)
            out[...] = value.astype(BF)

    return pl.pallas_call(
        kernel,
        in_specs=[SMEM, VMEM, ANY] + [VMEM] * k,
        out_specs=[VMEM] * n,
        out_shape=[jax.ShapeDtypeStruct((rows, w), BF) for w in widths],
        scratch_shapes=[pltpu.VMEM((hid, sum(widths)), BF), pltpu.SemaphoreType.DMA((n,))],
        compiler_params=PARAMS,
        cost_estimate=cost(
            2 * rows * hid * sum(widths), 2 * (rows * hid + sum(widths) * (hid + rows * (1 + k)))
        ),
        name="down",
    )(offsets, hidden, w_down, *addends)


def combine(spread, parts, toks):
    widths = [p.shape[1] for p in parts]

    def kernel(spread_ref, *refs):
        start = 0
        for ref, width in zip(refs[:-1], widths):
            both = dot(spread_ref[...], ref[...])
            refs[-1][:, start : start + width] = (both[:toks] + both[toks:]).astype(BF)
            start += width

    return pl.pallas_call(
        kernel,
        in_specs=[VMEM] * (1 + len(parts)),
        out_specs=VMEM,
        out_shape=jax.ShapeDtypeStruct((toks, sum(widths)), BF),
        compiler_params=PARAMS,
        name="combine",
    )(spread, *parts)


def on_device(tokens, routing, gate_weights, w_gate, w_up, w_down):
    toks, width = tokens.shape
    fanout = routing.shape[1]
    experts = lax.axis_size(ED)
    sections = lax.axis_size("section")
    cap = min(toks, max(2, 2 * toks * fanout // experts))
    quarter = width // sections
    s = lax.axis_index("section").astype(jnp.int32)
    right = [(k, (k + 1) % sections) for k in range(sections)]
    left = [(k, (k - 1) % sections) for k in range(sections)]

    def to_right(v):
        return lax.ppermute(v, "section", right)

    def to_left(v):
        return lax.ppermute(v, "section", left)

    def exchange(v):
        rows, w = v.shape
        return lax.all_to_all(
            v.reshape(experts, cap, w), ED, split_axis=0, concat_axis=0, tiled=True
        ).reshape(rows, w)

    def places(*pairs):
        return jnp.stack([lax.rem(s + d, sections) * quarter + c for d, c in pairs])

    o1, o2 = 0, OUT_WIDTHS[0]
    out1, out2, spread = make_slots(
        s.reshape(1), tokens, routing, gate_weights, cap, experts, OUT_WIDTHS
    )
    got1 = exchange(out1)
    got2 = exchange(tie(out2, got1))
    r1 = to_right(got1)
    l1 = to_left(got1)
    rr1 = to_right(r1)
    got2 = tie(got2, r1, l1)
    l2 = to_left(got2)
    r2 = to_right(got2)
    ll2 = to_left(l2)
    total = gate_up(places((0, o1), (3, o1), (1, o1)), (got1, r1, l1), w_gate, w_up)
    total = gate_up(places((2, o1), (0, o2), (1, o2)), (rr1, got2, l2), w_gate, w_up, total)
    b1, b2 = 0, BACK_WIDTHS[0]
    w1, w2 = BACK_WIDTHS
    hidden, far1, near1 = gate_up(
        places((3, o2), (2, o2)),
        (r2, ll2),
        w_gate,
        w_up,
        total,
        (w_down, places((2, b1), (3, b1)), (w1, w1)),
    )
    far1 = to_right(far1)
    near1 = to_left(near1)
    far2, near2 = project(places((2, b2), (1, b2)), (w2, w2), hidden, w_down)
    far2 = to_left(far2)
    (relay1,) = project(places((1, b1)), (w1,), hidden, w_down, (far1,))
    relay1 = to_right(relay1)
    near2 = to_right(tie(near2, relay1))
    (sum1,) = project(places((0, b1)), (w1,), hidden, w_down, (near1, relay1))
    back1 = exchange(sum1)
    (relay2,) = project(places((3, b2)), (w2,), hidden, w_down, (far2,))
    relay2 = to_left(relay2)
    (sum2,) = project(places((0, b2)), (w2,), hidden, w_down, (near2, relay2))
    back2 = exchange(sum2)
    return combine(spread, (back1, back2), toks)


def solution(mesh):
    placed = (
        P(ED, None),
        P(ED, None),
        P(ED, None),
        P(ED, None, "section"),
        P(ED, None, "section"),
        P(ED, "section", None),
    )
    return jax.shard_map(
        on_device,
        mesh=mesh,
        in_specs=placed,
        out_specs=P(ED, "section"),
        check_vma=False,
    )
```

```python
import jax
import jax.numpy as jnp
from jax import lax
from jax.experimental import pallas as pl
from jax.experimental.pallas import tpu as pltpu
from jax.sharding import PartitionSpec as P

ED = ("expert", "dp")
BF = jnp.bfloat16
F32 = jnp.float32
SMEM = pl.BlockSpec(memory_space=pltpu.SMEM)
ANY = pl.BlockSpec(memory_space=pl.ANY)
PARAMS = pltpu.CompilerParams(vmem_limit_bytes=56 * 1024 * 1024)


def dot(a, b):
    return jnp.dot(a, b, preferred_element_type=F32)


def cost(flops, read):
    return pl.CostEstimate(flops=flops, bytes_accessed=read, transcendentals=0)


def tie(value, *others):
    return lax.optimization_barrier((value,) + others)[0]


def make_slots(section, tokens, routing, gate_weights, cap, experts, widths):
    toks, fanout = routing.shape
    slots = experts * cap
    quarter = sum(widths)

    def kernel(s_ref, routing_ref, weights_ref, tokens_ref, *outs):
        slot = lax.broadcasted_iota(jnp.int32, (toks, slots), 1)
        expert, order = lax.div(slot, cap), lax.rem(slot, cap)
        named = jnp.zeros((toks, slots), F32)
        weight = jnp.zeros((toks, slots), F32)
        for k in range(fanout):
            hit = routing_ref[:, k : k + 1] == expert
            named = jnp.where(hit, 1.0, named)
            weight = jnp.where(hit, weights_ref[:, k : k + 1], weight)
        before = (
            lax.broadcasted_iota(jnp.int32, (toks, toks), 0)
            > lax.broadcasted_iota(jnp.int32, (toks, toks), 1)
        )
        earlier = dot(jnp.where(before, 1.0, 0.0).astype(BF), named.astype(BF))
        place = jnp.where(earlier == order.astype(F32), named, 0.0)
        rows = lax.dot_general(
            place.astype(BF),
            tokens_ref[...],
            (((0,), (0,)), ((), ())),
            preferred_element_type=F32,
        ).astype(BF)
        start = 0
        for out, width in zip(outs, widths):
            out[...] = rows[:, start : start + width]
            start += width
        spread = place * weight
        high = spread.astype(BF)
        outs[-1][...] = jnp.concatenate([high, (spread - high.astype(F32)).astype(BF)], axis=0)

    return pl.pallas_call(
        kernel,
        grid_spec=pltpu.PrefetchScalarGridSpec(
            num_scalar_prefetch=1,
            grid=(1,),
            in_specs=[
                pl.BlockSpec((toks, fanout), lambda i, s: (0, 0)),
                pl.BlockSpec((toks, fanout), lambda i, s: (0, 0)),
                pl.BlockSpec((toks, quarter), lambda i, s: (0, s[0])),
            ],
            out_specs=[pl.BlockSpec((slots, w), lambda i, s: (0, 0)) for w in widths]
            + [pl.BlockSpec((2 * toks, slots), lambda i, s: (0, 0))],
        ),
        out_shape=[jax.ShapeDtypeStruct((slots, w), BF) for w in widths]
        + [jax.ShapeDtypeStruct((2 * toks, slots), BF)],
        compiler_params=PARAMS,
        cost_estimate=cost(2 * slots * toks * quarter, 2 * slots * quarter),
        name="slots",
    )(section, routing, gate_weights, tokens)


def split_down(section, w_down, sections):
    _, hid, width = w_down.shape
    quarter = width // sections
    count = sections - 1

    def kernel(s_ref, d_ref, *refs):
        outs, sem = refs[:count], refs[count]
        copies = []
        for d in range(count):
            start = pl.multiple_of(lax.rem(s_ref[0] + d + 1, sections) * quarter, 128)
            copies.append(
                pltpu.make_async_copy(d_ref.at[0, :, pl.ds(start, quarter)], outs[d], sem.at[d])
            )
        for c in copies:
            c.start()
        for c in copies:
            c.wait()

    return pl.pallas_call(
        kernel,
        in_specs=[SMEM, ANY],
        out_specs=[ANY] * count,
        out_shape=[jax.ShapeDtypeStruct((hid, quarter), BF)] * count,
        scratch_shapes=[pltpu.SemaphoreType.DMA((count,))],
        compiler_params=PARAMS,
        cost_estimate=cost(0, 4 * count * hid * quarter),
        name="split_down",
    )(section, w_down)


def on_device(tokens, routing, gate_weights, w_gate, w_up, w_down):
    toks, width = tokens.shape
    fanout = routing.shape[1]
    experts = lax.axis_size(ED)
    sections = lax.axis_size("section")
    cap = min(toks, max(2, 2 * toks * fanout // experts))
    quarter = width // sections
    s = lax.axis_index("section").astype(jnp.int32)

    def send(v, d):
        return lax.ppermute(v, "section", [(k, (k + d) % sections) for k in range(sections)])

    def to_right(v):
        return send(v, 1)

    def to_left(v):
        return send(v, sections - 1)

    def exchange(v):
        rows, w = v.shape
        return lax.all_to_all(
            v.reshape(experts, cap, w), ED, split_axis=0, concat_axis=0, tiled=True
        ).reshape(rows, w)

    def gather(a, b):
        r_a, l_b = to_right(a), to_left(b)
        b_later, a_later, _, _ = lax.optimization_barrier((b, a, r_a, l_b))
        rr_a, ll_b = to_right(r_a), to_left(l_b)
        r_b, l_a = to_right(b_later), to_left(a_later)
        return (r_a, r_b), (l_a, l_b), (rr_a, ll_b)

    cut = split_down(s.reshape(1), w_down, sections)
    downs = [send(c, d + 1) for d, c in enumerate(cut)]
    own_down = lax.dynamic_slice_in_dim(w_down[0], s * quarter, quarter, axis=1)

    outgoing, spread = make_slots(
        s.reshape(1), tokens, routing, gate_weights, cap, experts, (quarter,)
    )
    received = exchange(tie(outgoing, *cut))
    received, *downs = lax.optimization_barrier((received, *downs))
    rows = experts * cap
    half = rows // 2

    def k_part(halves, d):
        block = jnp.concatenate(halves, axis=0)
        start = lax.rem(s + d, sections) * quarter
        g = lax.dynamic_slice_in_dim(w_gate[0], start, quarter, axis=0)
        u = lax.dynamic_slice_in_dim(w_up[0], start, quarter, axis=0)
        return dot(block, g), dot(block, u)

    own = (received[:half], received[half:])
    gate, up = k_part(own, 0)
    for halves, d in zip(gather(*own), (3, 1, 2)):
        g, u = k_part(halves, d)
        gate, up = gate + g, up + u
    hidden = (jax.nn.silu(gate) * up).astype(BF)
    out = dot(hidden, own_down)
    for d, down in enumerate(downs):
        out = out + dot(send(hidden, d + 1), down)
    returned = exchange(out.astype(BF))
    both = dot(spread, returned)
    return (both[:toks] + both[toks:]).astype(BF)


def solution(mesh):
    placed = (
        P(ED, None),
        P(ED, None),
        P(ED, None),
        P(ED, None, "section"),
        P(ED, None, "section"),
        P(ED, "section", None),
    )
    return jax.shard_map(
        on_device,
        mesh=mesh,
        in_specs=placed,
        out_specs=P(ED, "section"),
        check_vma=False,
    )
```

```python
import jax
import jax.numpy as jnp
from jax import lax
from jax.experimental import pallas as pl
from jax.experimental.pallas import tpu as pltpu
from jax.sharding import PartitionSpec as P

ED = ("expert", "dp")
BF = jnp.bfloat16
F32 = jnp.float32
SMEM = pl.BlockSpec(memory_space=pltpu.SMEM)
ANY = pl.BlockSpec(memory_space=pl.ANY)
PARAMS = pltpu.CompilerParams(vmem_limit_bytes=56 * 1024 * 1024)


def dot(a, b):
    return jnp.dot(a, b, preferred_element_type=F32)


def cost(flops, read):
    return pl.CostEstimate(flops=flops, bytes_accessed=read, transcendentals=0)


def tie(value, *others):
    return lax.optimization_barrier((value,) + others)[0]


def make_slots(section, tokens, routing, gate_weights, cap, experts, widths):
    toks, fanout = routing.shape
    slots = experts * cap
    quarter = sum(widths)

    def kernel(s_ref, routing_ref, weights_ref, tokens_ref, *outs):
        slot = lax.broadcasted_iota(jnp.int32, (toks, slots), 1)
        expert, order = lax.div(slot, cap), lax.rem(slot, cap)
        named = jnp.zeros((toks, slots), F32)
        weight = jnp.zeros((toks, slots), F32)
        routes, gates = routing_ref[...].T, weights_ref[...].T
        for k in range(fanout):
            hit = routes[:, k : k + 1] == expert
            named = jnp.where(hit, 1.0, named)
            weight = jnp.where(hit, gates[:, k : k + 1], weight)
        before = (
            lax.broadcasted_iota(jnp.int32, (toks, toks), 0)
            > lax.broadcasted_iota(jnp.int32, (toks, toks), 1)
        )
        earlier = dot(jnp.where(before, 1.0, 0.0).astype(BF), named.astype(BF))
        place = jnp.where(earlier == order.astype(F32), named, 0.0)
        rows = lax.dot_general(
            place.astype(BF),
            tokens_ref[...],
            (((0,), (0,)), ((), ())),
            preferred_element_type=F32,
        ).astype(BF)
        start = 0
        for out, width in zip(outs, widths):
            out[...] = rows[:, start : start + width]
            start += width
        spread = place * weight
        high = spread.astype(BF)
        outs[-1][...] = jnp.concatenate([high, (spread - high.astype(F32)).astype(BF)], axis=0)

    return pl.pallas_call(
        kernel,
        grid_spec=pltpu.PrefetchScalarGridSpec(
            num_scalar_prefetch=1,
            grid=(1,),
            in_specs=[
                pl.BlockSpec((fanout, toks), lambda i, s: (0, 0)),
                pl.BlockSpec((fanout, toks), lambda i, s: (0, 0)),
                pl.BlockSpec((toks, quarter), lambda i, s: (0, s[0])),
            ],
            out_specs=[pl.BlockSpec((slots, w), lambda i, s: (0, 0)) for w in widths]
            + [pl.BlockSpec((2 * toks, slots), lambda i, s: (0, 0))],
        ),
        out_shape=[jax.ShapeDtypeStruct((slots, w), BF) for w in widths]
        + [jax.ShapeDtypeStruct((2 * toks, slots), BF)],
        compiler_params=PARAMS,
        cost_estimate=cost(2 * slots * toks * quarter, 2 * slots * quarter),
        name="slots",
    )(section, routing.T, gate_weights.T, tokens)


def split_down(section, w_down, sections):
    _, hid, width = w_down.shape
    quarter = width // sections
    count = sections - 1

    def kernel(s_ref, *refs):
        for src, out in zip(refs[:count], refs[count:]):
            out[...] = src[0]

    def columns(d):
        return pl.BlockSpec((1, hid, quarter), lambda i, at: (0, 0, lax.rem(at[0] + d, sections)))

    return pl.pallas_call(
        kernel,
        grid_spec=pltpu.PrefetchScalarGridSpec(
            num_scalar_prefetch=1,
            grid=(1,),
            in_specs=[columns(d + 1) for d in range(count)],
            out_specs=[pl.BlockSpec((hid, quarter), lambda i, at: (0, 0))] * count,
        ),
        out_shape=[jax.ShapeDtypeStruct((hid, quarter), BF)] * count,
        compiler_params=PARAMS,
        cost_estimate=cost(0, 4 * count * hid * quarter),
        name="split_down",
    )(section, *([w_down] * count))


def project(section, hiddens, downs, w_down, sections):
    rows, hid = hiddens[0].shape
    quarter = downs[0].shape[1]
    n = len(hiddens)
    tile = rows // 2

    def kernel(s_ref, *refs):
        hs, ws, out = refs[:n], refs[n : 2 * n], refs[2 * n]

        def body(i, carry):
            at = pl.ds(pl.multiple_of(i * tile, tile), tile)
            total = dot(hs[0][at, :], ws[0][0])
            for h, w in zip(hs[1:], ws[1:]):
                total = total + dot(h[at, :], w[...])
            out[at, :] = total.astype(BF)
            return carry

        lax.fori_loop(0, rows // tile, body, 0)

    return pl.pallas_call(
        kernel,
        grid_spec=pltpu.PrefetchScalarGridSpec(
            num_scalar_prefetch=1,
            grid=(1,),
            in_specs=[pl.BlockSpec((rows, hid), lambda i, at: (0, 0))] * n
            + [pl.BlockSpec((1, hid, quarter), lambda i, at: (0, 0, at[0]))]
            + [pl.BlockSpec((hid, quarter), lambda i, at: (0, 0))] * (n - 1),
            out_specs=pl.BlockSpec((rows, quarter), lambda i, at: (0, 0)),
        ),
        out_shape=jax.ShapeDtypeStruct((rows, quarter), BF),
        compiler_params=PARAMS,
        cost_estimate=cost(2 * rows * hid * quarter * n, 2 * n * hid * (rows + quarter)),
        name="down",
    )(section, *hiddens, w_down, *downs)


def on_device(tokens, routing, gate_weights, w_gate, w_up, w_down):
    toks, width = tokens.shape
    fanout = routing.shape[1]
    experts = lax.axis_size(ED)
    sections = lax.axis_size("section")
    cap = min(toks, max(2, 2 * toks * fanout // experts))
    quarter = width // sections
    s = lax.axis_index("section").astype(jnp.int32)

    def send(v, d):
        return lax.ppermute(v, "section", [(k, (k + d) % sections) for k in range(sections)])

    def to_right(v):
        return send(v, 1)

    def to_left(v):
        return send(v, sections - 1)

    def exchange(v):
        rows, w = v.shape
        return lax.all_to_all(
            v.reshape(experts, cap, w), ED, split_axis=0, concat_axis=0, tiled=True
        ).reshape(rows, w)

    cut = split_down(s.reshape(1), w_down, sections)
    downs = [send(c, d + 1) for d, c in enumerate(cut)]
    outgoing, spread = make_slots(
        s.reshape(1), tokens, routing, gate_weights, cap, experts, (quarter,)
    )
    received = exchange(tie(outgoing, *cut))
    rows = experts * cap
    half = rows // 2

    def k_part(halves, d):
        block = jnp.concatenate(halves, axis=0)
        start = lax.rem(s + d, sections) * quarter
        g = lax.dynamic_slice_in_dim(w_gate[0], start, quarter, axis=0)
        u = lax.dynamic_slice_in_dim(w_up[0], start, quarter, axis=0)
        return dot(block, g), dot(block, u)

    a, b = received[:half], received[half:]
    r_a, l_b = to_right(a), to_left(b)
    gate, up = k_part((a, b), 0)
    a_later, b_later, gate, up, *downs = lax.optimization_barrier((a, b, gate, up, *downs))
    r_b, l_a = to_right(b_later), to_left(a_later)
    across = (to_right(r_a), to_left(l_b))
    for halves, d in (((r_a, r_b), 3), ((l_a, l_b), 1), (across, 2)):
        g, u = k_part(halves, d)
        gate, up = gate + g, up + u
    hidden = (jax.nn.silu(gate) * up).astype(BF)
    hiddens = [hidden] + [send(hidden, d + 1) for d in range(len(downs))]
    returned = exchange(project(s.reshape(1), hiddens, downs, w_down, sections))
    both = dot(spread, returned)
    return (both[:toks] + both[toks:]).astype(BF)


def solution(mesh):
    placed = (
        P(ED, None),
        P(ED, None),
        P(ED, None),
        P(ED, None, "section"),
        P(ED, None, "section"),
        P(ED, "section", None),
    )
    return jax.shard_map(
        on_device,
        mesh=mesh,
        in_specs=placed,
        out_specs=P(ED, "section"),
        check_vma=False,
    )
```

```python
import jax
import jax.numpy as jnp
from jax import lax
from jax.experimental import pallas as pl
from jax.experimental.pallas import tpu as pltpu
from jax.sharding import PartitionSpec as P

ED = ("expert", "dp")
BF = jnp.bfloat16
F32 = jnp.float32
SMEM = pl.BlockSpec(memory_space=pltpu.SMEM)
ANY = pl.BlockSpec(memory_space=pl.ANY)
PARAMS = pltpu.CompilerParams(vmem_limit_bytes=56 * 1024 * 1024)


def dot(a, b):
    return jnp.dot(a, b, preferred_element_type=F32)


def cost(flops, read):
    return pl.CostEstimate(flops=flops, bytes_accessed=read, transcendentals=0)


def tie(value, *others):
    return lax.optimization_barrier((value,) + others)[0]


def make_slots(section, tokens, routing, gate_weights, cap, experts, share):
    toks, fanout = routing.shape
    slots = experts * cap
    width = tokens.shape[1]
    tail = width - share * (width // share)

    def kernel(s_ref, routing_ref, weights_ref, *refs):
        sources, outs = refs[:2], refs[2:]
        slot = lax.broadcasted_iota(jnp.int32, (toks, slots), 1)
        expert, order = lax.div(slot, cap), lax.rem(slot, cap)
        named = jnp.zeros((toks, slots), F32)
        weight = jnp.zeros((toks, slots), F32)
        routes, gates = routing_ref[...].T, weights_ref[...].T
        for k in range(fanout):
            hit = routes[:, k : k + 1] == expert
            named = jnp.where(hit, 1.0, named)
            weight = jnp.where(hit, gates[:, k : k + 1], weight)
        before = (
            lax.broadcasted_iota(jnp.int32, (toks, toks), 0)
            > lax.broadcasted_iota(jnp.int32, (toks, toks), 1)
        )
        earlier = dot(jnp.where(before, 1.0, 0.0).astype(BF), named.astype(BF))
        place = jnp.where(earlier == order.astype(F32), named, 0.0)
        for source, out in zip(sources, outs):
            out[...] = lax.dot_general(
                place.astype(BF),
                source[...],
                (((0,), (0,)), ((), ())),
                preferred_element_type=F32,
            ).astype(BF)
        spread = place * weight
        high = spread.astype(BF)
        outs[-1][...] = jnp.concatenate([high, (spread - high.astype(F32)).astype(BF)], axis=0)

    return pl.pallas_call(
        kernel,
        grid_spec=pltpu.PrefetchScalarGridSpec(
            num_scalar_prefetch=1,
            grid=(1,),
            in_specs=[
                pl.BlockSpec((fanout, toks), lambda i, s: (0, 0)),
                pl.BlockSpec((fanout, toks), lambda i, s: (0, 0)),
                pl.BlockSpec((toks, share), lambda i, s: (0, s[0])),
                pl.BlockSpec((toks, tail), lambda i, s: (0, width // tail - 1)),
            ],
            out_specs=[pl.BlockSpec((slots, w), lambda i, s: (0, 0)) for w in (share, tail)]
            + [pl.BlockSpec((2 * toks, slots), lambda i, s: (0, 0))],
        ),
        out_shape=[jax.ShapeDtypeStruct((slots, w), BF) for w in (share, tail)]
        + [jax.ShapeDtypeStruct((2 * toks, slots), BF)],
        compiler_params=PARAMS,
        cost_estimate=cost(2 * slots * toks * (share + tail), 2 * slots * (share + tail)),
        name="slots",
    )(section, routing.T, gate_weights.T, tokens, tokens)


def split_down(section, w_down, sections):
    _, hid, width = w_down.shape
    quarter = width // sections
    count = sections - 1

    def kernel(s_ref, *refs):
        for src, out in zip(refs[:count], refs[count:]):
            out[...] = src[0]

    def columns(d):
        return pl.BlockSpec((1, hid, quarter), lambda i, at: (0, 0, lax.rem(at[0] + d, sections)))

    return pl.pallas_call(
        kernel,
        grid_spec=pltpu.PrefetchScalarGridSpec(
            num_scalar_prefetch=1,
            grid=(1,),
            in_specs=[columns(d + 1) for d in range(count)],
            out_specs=[pl.BlockSpec((hid, quarter), lambda i, at: (0, 0))] * count,
        ),
        out_shape=[jax.ShapeDtypeStruct((hid, quarter), BF)] * count,
        compiler_params=PARAMS,
        cost_estimate=cost(0, 4 * count * hid * quarter),
        name="split_down",
    )(section, *([w_down] * count))


def project(section, hiddens, downs, w_down, sections):
    rows, hid = hiddens[0].shape
    quarter = downs[0].shape[1]
    n = len(hiddens)
    tile = min(256, quarter)
    tiles = quarter // tile

    def kernel(s_ref, *refs):
        hs, ws, out = refs[:n], refs[n : 2 * n], refs[2 * n]
        total = dot(hs[0][...], ws[0][0])
        for h, w in zip(hs[1:], ws[1:]):
            total = total + dot(h[...], w[...])
        out[...] = total.astype(BF)

    return pl.pallas_call(
        kernel,
        grid_spec=pltpu.PrefetchScalarGridSpec(
            num_scalar_prefetch=1,
            grid=(tiles,),
            in_specs=[pl.BlockSpec((rows, hid), lambda i, at: (0, 0))] * n
            + [pl.BlockSpec((1, hid, tile), lambda i, at: (0, 0, at[0] * tiles + i))]
            + [pl.BlockSpec((hid, tile), lambda i, at: (0, i))] * (n - 1),
            out_specs=pl.BlockSpec((rows, tile), lambda i, at: (0, i)),
        ),
        out_shape=jax.ShapeDtypeStruct((rows, quarter), BF),
        compiler_params=PARAMS,
        cost_estimate=cost(2 * rows * hid * quarter * n, 2 * n * hid * (rows + quarter)),
        name="down",
    )(section, *hiddens, w_down, *downs)


def on_device(tokens, routing, gate_weights, w_gate, w_up, w_down):
    toks, width = tokens.shape
    fanout = routing.shape[1]
    experts = lax.axis_size(ED)
    sections = lax.axis_size("section")
    cap = min(toks, max(2, 2 * toks * fanout // experts))
    quarter = width // sections
    s = lax.axis_index("section").astype(jnp.int32)

    def send(v, d):
        return lax.ppermute(v, "section", [(k, (k + d) % sections) for k in range(sections)])

    def to_right(v):
        return send(v, 1)

    def to_left(v):
        return send(v, sections - 1)

    def exchange(v):
        rows, w = v.shape
        return lax.all_to_all(
            v.reshape(experts, cap, w), ED, split_axis=0, concat_axis=0, tiled=True
        ).reshape(rows, w)

    cut = split_down(s.reshape(1), w_down, sections)
    downs = [send(c, d + 1) for d, c in enumerate(cut)]
    share = quarter - quarter // 8
    outgoing, straight, spread = make_slots(
        s.reshape(1), tokens, routing, gate_weights, cap, experts, share
    )
    received = exchange(tie(outgoing, *cut))
    rows = experts * cap
    half = rows // 2

    def k_rows(block, start):
        g = lax.dynamic_slice_in_dim(w_gate[0], start, block.shape[1], axis=0)
        u = lax.dynamic_slice_in_dim(w_up[0], start, block.shape[1], axis=0)
        return dot(block, g), dot(block, u)

    def k_part(halves, d):
        return k_rows(jnp.concatenate(halves, axis=0), lax.rem(s + d, sections) * share)

    a, b = received[:half], received[half:]
    r_a, l_b = to_right(a), to_left(b)
    gate, up = k_part((a, b), 0)
    a_later, b_later, straight, gate, up, *downs = lax.optimization_barrier(
        (a, b, straight, gate, up, *downs)
    )
    r_b, l_a = to_right(b_later), to_left(a_later)
    across = (to_right(r_a), to_left(l_b))
    straight = exchange(straight)
    parts = [k_part(halves, d) for halves, d in (((r_a, r_b), 3), ((l_a, l_b), 1))]
    parts.append(k_rows(straight, share * sections))
    parts.append(k_part(across, 2))
    for g, u in parts:
        gate, up = gate + g, up + u
    hidden = (jax.nn.silu(gate) * up).astype(BF)
    hiddens = [hidden] + [send(hidden, d + 1) for d in range(len(downs))]
    returned = exchange(project(s.reshape(1), hiddens, downs, w_down, sections))
    both = dot(spread, returned)
    return (both[:toks] + both[toks:]).astype(BF)


def solution(mesh):
    placed = (
        P(ED, None),
        P(ED, None),
        P(ED, None),
        P(ED, None, "section"),
        P(ED, None, "section"),
        P(ED, "section", None),
    )
    return jax.shard_map(
        on_device,
        mesh=mesh,
        in_specs=placed,
        out_specs=P(ED, "section"),
        check_vma=False,
    )
```

```python
import jax
import jax.numpy as jnp
from jax import lax
from jax.experimental import pallas as pl
from jax.experimental.pallas import tpu as pltpu
from jax.sharding import PartitionSpec as P

ED = ("expert", "dp")
BF = jnp.bfloat16
F32 = jnp.float32
SMEM = pl.BlockSpec(memory_space=pltpu.SMEM)
ANY = pl.BlockSpec(memory_space=pl.ANY)
PARAMS = pltpu.CompilerParams(vmem_limit_bytes=56 * 1024 * 1024)


def dot(a, b):
    return jnp.dot(a, b, preferred_element_type=F32)


def cost(flops, read):
    return pl.CostEstimate(flops=flops, bytes_accessed=read, transcendentals=0)


def tie(value, *others):
    return lax.optimization_barrier((value,) + others)[0]


def make_slots(section, tokens, routing, gate_weights, cap, experts, share):
    toks, fanout = routing.shape
    slots = experts * cap
    width = tokens.shape[1]
    tail = width - share * (width // share)

    def kernel(s_ref, routing_ref, weights_ref, *refs):
        sources, outs = refs[:2], refs[2:]
        slot = lax.broadcasted_iota(jnp.int32, (toks, slots), 1)
        expert, order = lax.div(slot, cap), lax.rem(slot, cap)
        named = jnp.zeros((toks, slots), F32)
        weight = jnp.zeros((toks, slots), F32)
        routes, gates = routing_ref[...].T, weights_ref[...].T
        for k in range(fanout):
            hit = routes[:, k : k + 1] == expert
            named = jnp.where(hit, 1.0, named)
            weight = jnp.where(hit, gates[:, k : k + 1], weight)
        before = (
            lax.broadcasted_iota(jnp.int32, (toks, toks), 0)
            > lax.broadcasted_iota(jnp.int32, (toks, toks), 1)
        )
        earlier = dot(jnp.where(before, 1.0, 0.0).astype(BF), named.astype(BF))
        place = jnp.where(earlier == order.astype(F32), named, 0.0)
        for source, out in zip(sources, outs):
            out[...] = lax.dot_general(
                place.astype(BF),
                source[...],
                (((0,), (0,)), ((), ())),
                preferred_element_type=F32,
            ).astype(BF)
        spread = place * weight
        high = spread.astype(BF)
        outs[-1][...] = jnp.concatenate([high, (spread - high.astype(F32)).astype(BF)], axis=0)

    return pl.pallas_call(
        kernel,
        grid_spec=pltpu.PrefetchScalarGridSpec(
            num_scalar_prefetch=1,
            grid=(1,),
            in_specs=[
                pl.BlockSpec((fanout, toks), lambda i, s: (0, 0)),
                pl.BlockSpec((fanout, toks), lambda i, s: (0, 0)),
                pl.BlockSpec((toks, share), lambda i, s: (0, s[0])),
                pl.BlockSpec((toks, tail), lambda i, s: (0, width // tail - 1)),
            ],
            out_specs=[pl.BlockSpec((slots, w), lambda i, s: (0, 0)) for w in (share, tail)]
            + [pl.BlockSpec((2 * toks, slots), lambda i, s: (0, 0))],
        ),
        out_shape=[jax.ShapeDtypeStruct((slots, w), BF) for w in (share, tail)]
        + [jax.ShapeDtypeStruct((2 * toks, slots), BF)],
        compiler_params=PARAMS,
        cost_estimate=cost(2 * slots * toks * (share + tail), 2 * slots * (share + tail)),
        name="slots",
    )(section, routing.T, gate_weights.T, tokens, tokens)


def split_down(section, w_down, pieces, sections):
    _, hid, width = w_down.shape
    quarter = width // sections
    count = len(pieces)

    def kernel(s_ref, *refs):
        for src, out in zip(refs[:count], refs[count:]):
            out[...] = src[0]

    def columns(d, part, parts):
        return pl.BlockSpec(
            (1, hid // parts, quarter), lambda i, at: (0, part, lax.rem(at[0] + d, sections))
        )

    return pl.pallas_call(
        kernel,
        grid_spec=pltpu.PrefetchScalarGridSpec(
            num_scalar_prefetch=1,
            grid=(1,),
            in_specs=[columns(*p) for p in pieces],
            out_specs=[
                pl.BlockSpec((hid // parts, quarter), lambda i, at: (0, 0)) for _, _, parts in pieces
            ],
        ),
        out_shape=[jax.ShapeDtypeStruct((hid // parts, quarter), BF) for _, _, parts in pieces],
        compiler_params=PARAMS,
        cost_estimate=cost(0, 4 * (sections - 1) * hid * quarter),
        name="split_down",
    )(section, *([w_down] * count))


def gate_up(section, blocks, starts, w_gate, w_up, sections, total=None, last=False):
    rows = sum(p.shape[0] for p in blocks[0])
    hid = w_gate.shape[2]
    n = len(blocks)
    flat = [p for parts in blocks for p in parts]
    counts = [len(parts) for parts in blocks]
    widths = [parts[0].shape[1] for parts in blocks]

    def kernel(s_ref, *refs):
        refs = list(refs)
        xs = [[refs.pop(0) for _ in range(c)] for c in counts]
        gs = [refs.pop(0) for _ in range(n)]
        us = [refs.pop(0) for _ in range(n)]
        acc = refs.pop(0)[...] if total is not None else None
        for x, g, u in zip(xs, gs, us):
            block = x[0][...] if len(x) == 1 else jnp.concatenate([p[...] for p in x], axis=0)
            term = dot(block, jnp.concatenate([g[0], u[0]], axis=1))
            acc = term if acc is None else acc + term
        if not last:
            refs[0][...] = acc
            return
        gate, up = acc[:, :hid], acc[:, hid:]
        refs[0][...] = (gate / (1.0 + jnp.exp(-gate)) * up).astype(BF)

    def weights(start, width):
        if isinstance(start, tuple):
            return pl.BlockSpec(
                (1, width, hid), lambda i, at: (0, lax.rem(at[0] + start[0], sections), 0)
            )
        return pl.BlockSpec((1, width, hid), lambda i, at: (0, start, 0))

    def whole(v):
        return pl.BlockSpec(v.shape, lambda i, at: (0, 0))

    w_specs = [weights(st, w) for st, w in zip(starts, widths)]
    extra = [] if total is None else [total]
    shape = jax.ShapeDtypeStruct((rows, hid), BF) if last else jax.ShapeDtypeStruct((rows, 2 * hid), F32)
    return pl.pallas_call(
        kernel,
        grid_spec=pltpu.PrefetchScalarGridSpec(
            num_scalar_prefetch=1,
            grid=(1,),
            in_specs=[whole(v) for v in flat] + w_specs + w_specs + [whole(v) for v in extra],
            out_specs=whole(shape),
        ),
        out_shape=shape,
        compiler_params=PARAMS,
        cost_estimate=cost(
            4 * rows * hid * sum(widths), 2 * sum(widths) * (rows + 2 * hid) + 8 * rows * hid
        ),
        name="gate_up",
    )(section, *flat, *([w_gate] * n), *([w_up] * n), *extra)


def project(section, hiddens, downs, w_down, sections):
    rows, hid = hiddens[0].shape
    quarter = downs[0].shape[1]
    n = len(hiddens)
    tile = min(256, quarter)
    tiles = quarter // tile

    def kernel(s_ref, *refs):
        hs, ws, out = refs[:n], refs[n:-1], refs[-1]
        hidden = jnp.concatenate([h[...] for h in hs], axis=1)
        columns = jnp.concatenate([ws[0][0]] + [w[...] for w in ws[1:]], axis=0)
        out[...] = dot(hidden, columns).astype(BF)

    return pl.pallas_call(
        kernel,
        grid_spec=pltpu.PrefetchScalarGridSpec(
            num_scalar_prefetch=1,
            grid=(tiles,),
            in_specs=[pl.BlockSpec((rows, hid), lambda i, at: (0, 0))] * n
            + [pl.BlockSpec((1, hid, tile), lambda i, at: (0, 0, at[0] * tiles + i))]
            + [pl.BlockSpec((d.shape[0], tile), lambda i, at: (0, i)) for d in downs],
            out_specs=pl.BlockSpec((rows, tile), lambda i, at: (0, i)),
        ),
        out_shape=jax.ShapeDtypeStruct((rows, quarter), BF),
        compiler_params=PARAMS,
        cost_estimate=cost(2 * rows * hid * quarter * n, 2 * n * hid * (rows + quarter)),
        name="down",
    )(section, *hiddens, w_down, *downs)


def on_device(tokens, routing, gate_weights, w_gate, w_up, w_down):
    toks, width = tokens.shape
    fanout = routing.shape[1]
    experts = lax.axis_size(ED)
    sections = lax.axis_size("section")
    cap = min(toks, max(2, 2 * toks * fanout // experts))
    quarter = width // sections
    s = lax.axis_index("section").astype(jnp.int32)

    def send(v, d):
        return lax.ppermute(v, "section", [(k, (k + d) % sections) for k in range(sections)])

    def to_right(v):
        return send(v, 1)

    def to_left(v):
        return send(v, sections - 1)

    def exchange(v):
        rows, w = v.shape
        return lax.all_to_all(
            v.reshape(experts, cap, w), ED, split_axis=0, concat_axis=0, tiled=True
        ).reshape(rows, w)

    pieces = [(1, 0, 1), (2, 0, 2), (2, 1, 2), (3, 0, 1)]
    cut = split_down(s.reshape(1), w_down, pieces, sections)
    downs = [send(c, p[0]) for c, p in zip(cut, pieces)]

    share = quarter - quarter // 8
    outgoing, straight, spread = make_slots(
        s.reshape(1), tokens, routing, gate_weights, cap, experts, share
    )
    received = exchange(tie(outgoing, *cut))
    rows = experts * cap
    half = rows // 2

    straight, received, downs[0], downs[1], downs[3] = lax.optimization_barrier(
        (straight, received, downs[0], downs[1], downs[3])
    )
    from_left, from_right = to_right(received), to_left(received)
    straight = exchange(straight)
    at = s.reshape(1)
    total = gate_up(at, [(received,)], [(0,)], w_gate, w_up, sections)
    from_left, from_right, total, *downs = lax.optimization_barrier(
        (from_left, from_right, total, *downs)
    )
    pass_r, pass_l = from_left[:half], from_right[half:]
    across = (to_right(pass_r), to_left(pass_l))
    from_left, from_right, pass_r, pass_l = lax.optimization_barrier(
        (from_left, from_right, pass_r, pass_l)
    )
    total = gate_up(
        at,
        [(from_left,), (from_right,)],
        [(sections - 1,), (1,)],
        w_gate,
        w_up,
        sections,
        total,
    )
    hidden = gate_up(
        at,
        [(straight,), across],
        [width // straight.shape[1] - 1, (2,)],
        w_gate,
        w_up,
        sections,
        total,
        last=True,
    )
    hiddens = [hidden] + [send(hidden, d) for d in range(1, sections)]
    returned = exchange(project(s.reshape(1), hiddens, downs, w_down, sections))
    both = dot(spread, returned)
    return (both[:toks] + both[toks:]).astype(BF)


def solution(mesh):
    placed = (
        P(ED, None),
        P(ED, None),
        P(ED, None),
        P(ED, None, "section"),
        P(ED, None, "section"),
        P(ED, "section", None),
    )
    return jax.shard_map(
        on_device,
        mesh=mesh,
        in_specs=placed,
        out_specs=P(ED, "section"),
        check_vma=False,
    )
```

```python
import jax
import jax.numpy as jnp
from jax import lax
from jax.experimental import pallas as pl
from jax.experimental.pallas import tpu as pltpu
from jax.sharding import PartitionSpec as P

ED = ("expert", "dp")
BF = jnp.bfloat16
F32 = jnp.float32
ANY = pl.BlockSpec(memory_space=pl.ANY)
PARAMS = pltpu.CompilerParams(vmem_limit_bytes=56 * 1024 * 1024)


def dot(a, b):
    return jnp.dot(a, b, preferred_element_type=F32)


def cost(flops, read):
    return pl.CostEstimate(flops=flops, bytes_accessed=read, transcendentals=0)


def first(section, tokens, routing, gate_weights, w_down, cap, experts, sections):
    toks, fanout = routing.shape
    slots = experts * cap
    _, hid, width = w_down.shape
    quarter = width // sections
    count = sections - 1

    def kernel(s_ref, routing_ref, weights_ref, tokens_ref, down_ref, *refs):
        rows_ref, spread_ref = refs[:2]
        cuts, bufs = refs[2 : 2 + count], refs[2 + count]
        in_sem, out_sem = refs[3 + count], refs[4 + count]
        ins, outs = [], []
        for d in range(count):
            start = pl.multiple_of(lax.rem(s_ref[0] + d + 1, sections) * quarter, 128)
            ins.append(
                pltpu.make_async_copy(
                    down_ref.at[0, :, pl.ds(start, quarter)], bufs.at[d], in_sem.at[d]
                )
            )
            outs.append(pltpu.make_async_copy(bufs.at[d], cuts[d], out_sem.at[d]))
        for c in ins:
            c.start()
        slot = lax.broadcasted_iota(jnp.int32, (toks, slots), 1)
        expert, order = lax.div(slot, cap), lax.rem(slot, cap)
        named = jnp.zeros((toks, slots), F32)
        weight = jnp.zeros((toks, slots), F32)
        routes, gates = routing_ref[...].T, weights_ref[...].T
        for k in range(fanout):
            hit = routes[:, k : k + 1] == expert
            named = jnp.where(hit, 1.0, named)
            weight = jnp.where(hit, gates[:, k : k + 1], weight)
        for c_in, c_out in zip(ins, outs):
            c_in.wait()
            c_out.start()
        before = (
            lax.broadcasted_iota(jnp.int32, (toks, toks), 0)
            > lax.broadcasted_iota(jnp.int32, (toks, toks), 1)
        )
        earlier = dot(jnp.where(before, 1.0, 0.0).astype(BF), named.astype(BF))
        place = jnp.where(earlier == order.astype(F32), named, 0.0)
        rows_ref[...] = lax.dot_general(
            place.astype(BF),
            tokens_ref[...],
            (((0,), (0,)), ((), ())),
            preferred_element_type=F32,
        ).astype(BF)
        spread = place * weight
        high = spread.astype(BF)
        spread_ref[...] = jnp.concatenate([high, (spread - high.astype(F32)).astype(BF)], axis=0)
        for c in outs:
            c.wait()

    def whole(*shape):
        return pl.BlockSpec(shape, lambda i, s: (0, 0))

    rows, spread, *cut = pl.pallas_call(
        kernel,
        grid_spec=pltpu.PrefetchScalarGridSpec(
            num_scalar_prefetch=1,
            grid=(1,),
            in_specs=[
                whole(fanout, toks),
                whole(fanout, toks),
                pl.BlockSpec((toks, quarter), lambda i, s: (0, s[0])),
                ANY,
            ],
            out_specs=[whole(slots, quarter), whole(2 * toks, slots)] + [ANY] * count,
            scratch_shapes=[
                pltpu.VMEM((count, hid, quarter), BF),
                pltpu.SemaphoreType.DMA((count,)),
                pltpu.SemaphoreType.DMA((count,)),
            ],
        ),
        out_shape=[
            jax.ShapeDtypeStruct((slots, quarter), BF),
            jax.ShapeDtypeStruct((2 * toks, slots), BF),
        ]
        + [jax.ShapeDtypeStruct((hid, quarter), BF)] * count,
        compiler_params=PARAMS,
        cost_estimate=cost(
            2 * slots * toks * quarter, 2 * slots * quarter + 4 * count * hid * quarter
        ),
        name="first",
    )(section, routing.T, gate_weights.T, tokens, w_down)
    return rows, spread, cut


def on_device(tokens, routing, gate_weights, w_gate, w_up, w_down):
    toks, width = tokens.shape
    fanout = routing.shape[1]
    experts = lax.axis_size(ED)
    sections = lax.axis_size("section")
    cap = min(toks, max(2, 2 * toks * fanout // experts))
    quarter = width // sections
    s = lax.axis_index("section").astype(jnp.int32)

    def send(v, d):
        return lax.ppermute(v, "section", [(k, (k + d) % sections) for k in range(sections)])

    def to_right(v):
        return send(v, 1)

    def to_left(v):
        return send(v, sections - 1)

    def exchange(v):
        rows, w = v.shape
        return lax.all_to_all(
            v.reshape(experts, cap, w), ED, split_axis=0, concat_axis=0, tiled=True
        ).reshape(rows, w)

    outgoing, spread, cut = first(
        s.reshape(1), tokens, routing, gate_weights, w_down, cap, experts, sections
    )
    downs = [send(c, d + 1) for d, c in enumerate(cut)]
    received = exchange(outgoing)
    rows = experts * cap
    half = rows // 2

    def k_part(halves, d):
        block = jnp.concatenate(halves, axis=0)
        start = lax.rem(s + d, sections) * quarter
        g = lax.dynamic_slice_in_dim(w_gate[0], start, quarter, axis=0)
        u = lax.dynamic_slice_in_dim(w_up[0], start, quarter, axis=0)
        return dot(block, g), dot(block, u)

    a, b = received[:half], received[half:]
    r_a, l_b = to_right(a), to_left(b)
    gate, up = k_part((a, b), 0)
    a_later, b_later, gate, up, *downs = lax.optimization_barrier((a, b, gate, up, *downs))
    r_b, l_a = to_right(b_later), to_left(a_later)
    across = (to_right(r_a), to_left(l_b))
    for halves, d in (((r_a, r_b), 3), ((l_a, l_b), 1), (across, 2)):
        g, u = k_part(halves, d)
        gate, up = gate + g, up + u
    hidden = (jax.nn.silu(gate) * up).astype(BF)
    out = dot(hidden, lax.dynamic_slice_in_dim(w_down[0], s * quarter, quarter, axis=1))
    for d, down in enumerate(downs):
        out = out + dot(send(hidden, d + 1), down)
    returned = exchange(out.astype(BF))
    both = dot(spread, returned)
    return (both[:toks] + both[toks:]).astype(BF)


def solution(mesh):
    placed = (
        P(ED, None),
        P(ED, None),
        P(ED, None),
        P(ED, None, "section"),
        P(ED, None, "section"),
        P(ED, "section", None),
    )
    return jax.shard_map(
        on_device,
        mesh=mesh,
        in_specs=placed,
        out_specs=P(ED, "section"),
        check_vma=False,
    )
```

```python
import jax
import jax.numpy as jnp
from jax import lax
from jax.experimental import pallas as pl
from jax.experimental.pallas import tpu as pltpu
from jax.sharding import PartitionSpec as P

ED = ("expert", "dp")
BF = jnp.bfloat16
F32 = jnp.float32
ANY = pl.BlockSpec(memory_space=pl.ANY)
PARAMS = pltpu.CompilerParams(vmem_limit_bytes=56 * 1024 * 1024)


def dot(a, b):
    return jnp.dot(a, b, preferred_element_type=F32)


def cost(flops, read):
    return pl.CostEstimate(flops=flops, bytes_accessed=read, transcendentals=0)


def first(section, tokens, routing, gate_weights, w_down, cap, experts, sections):
    toks, fanout = routing.shape
    slots = experts * cap
    _, hid, width = w_down.shape
    quarter = width // sections
    count = sections - 1

    def kernel(s_ref, routing_ref, weights_ref, tokens_ref, down_ref, *refs):
        rows_ref, spread_ref = refs[:2]
        cuts, bufs = refs[2 : 2 + count], refs[2 + count]
        in_sem, out_sem = refs[3 + count], refs[4 + count]
        ins, outs = [], []
        for d in range(count):
            start = pl.multiple_of(lax.rem(s_ref[0] + d + 1, sections) * quarter, 128)
            ins.append(
                pltpu.make_async_copy(
                    down_ref.at[0, :, pl.ds(start, quarter)], bufs.at[d], in_sem.at[d]
                )
            )
            outs.append(pltpu.make_async_copy(bufs.at[d], cuts[d], out_sem.at[d]))
        for c in ins:
            c.start()
        slot = lax.broadcasted_iota(jnp.int32, (slots, toks), 0)
        expert, order = lax.div(slot, cap), lax.rem(slot, cap)
        named = jnp.zeros((slots, toks), F32)
        weight = jnp.zeros((slots, toks), F32)
        for k in range(fanout):
            hit = routing_ref[k : k + 1, :] == expert
            named = jnp.where(hit, 1.0, named)
            weight = jnp.where(hit, weights_ref[k : k + 1, :], weight)
        for c_in, c_out in zip(ins, outs):
            c_in.wait()
            c_out.start()
        before = (
            lax.broadcasted_iota(jnp.int32, (toks, toks), 0)
            < lax.broadcasted_iota(jnp.int32, (toks, toks), 1)
        )
        earlier = dot(named.astype(BF), jnp.where(before, 1.0, 0.0).astype(BF))
        place = jnp.where(earlier == order.astype(F32), named, 0.0)
        rows_ref[...] = dot(place.astype(BF), tokens_ref[...]).astype(BF)
        spread = place * weight
        high = spread.astype(BF)
        spread_ref[...] = jnp.concatenate([high, (spread - high.astype(F32)).astype(BF)], axis=1)
        for c in outs:
            c.wait()

    def whole(*shape):
        return pl.BlockSpec(shape, lambda i, s: (0, 0))

    rows, spread, *cut = pl.pallas_call(
        kernel,
        grid_spec=pltpu.PrefetchScalarGridSpec(
            num_scalar_prefetch=1,
            grid=(1,),
            in_specs=[
                whole(fanout, toks),
                whole(fanout, toks),
                pl.BlockSpec((toks, quarter), lambda i, s: (0, s[0])),
                ANY,
            ],
            out_specs=[whole(slots, quarter), whole(slots, 2 * toks)] + [ANY] * count,
            scratch_shapes=[
                pltpu.VMEM((count, hid, quarter), BF),
                pltpu.SemaphoreType.DMA((count,)),
                pltpu.SemaphoreType.DMA((count,)),
            ],
        ),
        out_shape=[
            jax.ShapeDtypeStruct((slots, quarter), BF),
            jax.ShapeDtypeStruct((slots, 2 * toks), BF),
        ]
        + [jax.ShapeDtypeStruct((hid, quarter), BF)] * count,
        compiler_params=PARAMS,
        cost_estimate=cost(
            2 * slots * toks * quarter, 2 * slots * quarter + 4 * count * hid * quarter
        ),
        name="first",
    )(section, routing.T, gate_weights.T, tokens, w_down)
    return rows, spread, cut


def on_device(tokens, routing, gate_weights, w_gate, w_up, w_down):
    toks, width = tokens.shape
    fanout = routing.shape[1]
    experts = lax.axis_size(ED)
    sections = lax.axis_size("section")
    cap = min(toks, max(2, 2 * toks * fanout // experts))
    quarter = width // sections
    s = lax.axis_index("section").astype(jnp.int32)

    def send(v, d):
        return lax.ppermute(v, "section", [(k, (k + d) % sections) for k in range(sections)])

    def to_right(v):
        return send(v, 1)

    def to_left(v):
        return send(v, sections - 1)

    def exchange(v):
        rows, w = v.shape
        return lax.all_to_all(
            v.reshape(experts, cap, w), ED, split_axis=0, concat_axis=0, tiled=True
        ).reshape(rows, w)

    outgoing, spread, cut = first(
        s.reshape(1), tokens, routing, gate_weights, w_down, cap, experts, sections
    )
    downs = [send(c, d + 1) for d, c in enumerate(cut)]
    received = exchange(outgoing)
    rows = experts * cap
    half = rows // 2

    def k_part(halves, d):
        block = jnp.concatenate(halves, axis=0)
        start = lax.rem(s + d, sections) * quarter
        g = lax.dynamic_slice_in_dim(w_gate[0], start, quarter, axis=0)
        u = lax.dynamic_slice_in_dim(w_up[0], start, quarter, axis=0)
        return dot(block, g), dot(block, u)

    a, b = received[:half], received[half:]
    r_a, l_b = to_right(a), to_left(b)
    gate, up = k_part((a, b), 0)
    a_later, b_later, gate, up, *downs = lax.optimization_barrier((a, b, gate, up, *downs))
    r_b, l_a = to_right(b_later), to_left(a_later)
    across = (to_right(r_a), to_left(l_b))
    for halves, d in (((r_a, r_b), 3), ((l_a, l_b), 1), (across, 2)):
        g, u = k_part(halves, d)
        gate, up = gate + g, up + u
    hidden = (jax.nn.silu(gate) * up).astype(BF)
    near = [send(hidden, d) for d in (1, sections - 1)]
    out = dot(hidden, lax.dynamic_slice_in_dim(w_down[0], s * quarter, quarter, axis=1))
    far = send(lax.optimization_barrier((hidden, out))[0], 2)
    for block, down in zip(near, (downs[0], downs[2])):
        out = out + dot(block, down)
    out = out + dot(far, downs[1])
    returned = exchange(out.astype(BF))
    both = lax.dot_general(
        spread, returned, (((0,), (0,)), ((), ())), preferred_element_type=F32
    )
    return (both[:toks] + both[toks:]).astype(BF)


def solution(mesh):
    placed = (
        P(ED, None),
        P(ED, None),
        P(ED, None),
        P(ED, None, "section"),
        P(ED, None, "section"),
        P(ED, "section", None),
    )
    return jax.shard_map(
        on_device,
        mesh=mesh,
        in_specs=placed,
        out_specs=P(ED, "section"),
        check_vma=False,
    )
```

```python
import jax
import jax.numpy as jnp
from jax import lax
from jax.experimental import pallas as pl
from jax.experimental.pallas import tpu as pltpu
from jax.sharding import PartitionSpec as P

ED = ("expert", "dp")
BF = jnp.bfloat16
F32 = jnp.float32
ANY = pl.BlockSpec(memory_space=pl.ANY)
PARAMS = pltpu.CompilerParams(vmem_limit_bytes=56 * 1024 * 1024)


def dot(a, b):
    return jnp.dot(a, b, preferred_element_type=F32)


def cost(flops, read):
    return pl.CostEstimate(flops=flops, bytes_accessed=read, transcendentals=0)


def first(section, tokens, routing, gate_weights, w_down, cap, experts, sections):
    toks, fanout = routing.shape
    slots = experts * cap
    _, hid, width = w_down.shape
    quarter = width // sections
    count = sections - 1

    def kernel(s_ref, routing_ref, weights_ref, tokens_ref, down_ref, *refs):
        rows_ref, spread_ref = refs[:2]
        cuts, bufs = refs[2 : 2 + count], refs[2 + count]
        in_sem, out_sem = refs[3 + count], refs[4 + count]
        ins, outs = [], []
        for d in range(count):
            start = pl.multiple_of(lax.rem(s_ref[0] + d + 1, sections) * quarter, 128)
            ins.append(
                pltpu.make_async_copy(
                    down_ref.at[0, :, pl.ds(start, quarter)], bufs.at[d], in_sem.at[d]
                )
            )
            outs.append(pltpu.make_async_copy(bufs.at[d], cuts[d], out_sem.at[d]))
        for c in ins:
            c.start()
        slot = lax.broadcasted_iota(jnp.int32, (slots, toks), 0)
        expert, order = lax.div(slot, cap), lax.rem(slot, cap)
        named = jnp.zeros((slots, toks), F32)
        weight = jnp.zeros((slots, toks), F32)
        for k in range(fanout):
            hit = routing_ref[k : k + 1, :] == expert
            named = jnp.where(hit, 1.0, named)
            weight = jnp.where(hit, weights_ref[k : k + 1, :], weight)
        for c_in, c_out in zip(ins, outs):
            c_in.wait()
            c_out.start()
        before = (
            lax.broadcasted_iota(jnp.int32, (toks, toks), 0)
            < lax.broadcasted_iota(jnp.int32, (toks, toks), 1)
        )
        earlier = dot(named.astype(BF), jnp.where(before, 1.0, 0.0).astype(BF))
        place = jnp.where(earlier == order.astype(F32), named, 0.0)
        rows_ref[...] = dot(place.astype(BF), tokens_ref[...]).astype(BF)
        spread = place * weight
        high = spread.astype(BF)
        spread_ref[...] = jnp.concatenate([high, (spread - high.astype(F32)).astype(BF)], axis=1)
        for c in outs:
            c.wait()

    def whole(*shape):
        return pl.BlockSpec(shape, lambda i, s: (0, 0))

    rows, spread, *cut = pl.pallas_call(
        kernel,
        grid_spec=pltpu.PrefetchScalarGridSpec(
            num_scalar_prefetch=1,
            grid=(1,),
            in_specs=[
                whole(fanout, toks),
                whole(fanout, toks),
                pl.BlockSpec((toks, quarter), lambda i, s: (0, s[0])),
                ANY,
            ],
            out_specs=[whole(slots, quarter), whole(slots, 2 * toks)] + [ANY] * count,
            scratch_shapes=[
                pltpu.VMEM((count, hid, quarter), BF),
                pltpu.SemaphoreType.DMA((count,)),
                pltpu.SemaphoreType.DMA((count,)),
            ],
        ),
        out_shape=[
            jax.ShapeDtypeStruct((slots, quarter), BF),
            jax.ShapeDtypeStruct((slots, 2 * toks), BF),
        ]
        + [jax.ShapeDtypeStruct((hid, quarter), BF)] * count,
        compiler_params=PARAMS,
        cost_estimate=cost(
            2 * slots * toks * quarter, 2 * slots * quarter + 4 * count * hid * quarter
        ),
        name="first",
    )(section, routing.T, gate_weights.T, tokens, w_down)
    return rows, spread, cut


def on_device(tokens, routing, gate_weights, w_gate, w_up, w_down):
    toks, width = tokens.shape
    fanout = routing.shape[1]
    experts = lax.axis_size(ED)
    sections = lax.axis_size("section")
    cap = min(toks, max(2, 2 * toks * fanout // experts))
    quarter = width // sections
    s = lax.axis_index("section").astype(jnp.int32)

    def send(v, d):
        return lax.ppermute(v, "section", [(k, (k + d) % sections) for k in range(sections)])

    def to_right(v):
        return send(v, 1)

    def to_left(v):
        return send(v, sections - 1)

    def exchange(v):
        rows, w = v.shape
        return lax.all_to_all(
            v.reshape(experts, cap, w), ED, split_axis=0, concat_axis=0, tiled=True
        ).reshape(rows, w)

    outgoing, spread, cut = first(
        s.reshape(1), tokens, routing, gate_weights, w_down, cap, experts, sections
    )
    downs = [send(c, d + 1) for d, c in enumerate(cut)]
    received = exchange(outgoing)
    rows = experts * cap
    half = rows // 2

    def k_part(halves, d):
        block = jnp.concatenate(halves, axis=0)
        start = lax.rem(s + d, sections) * quarter
        g = lax.dynamic_slice_in_dim(w_gate[0], start, quarter, axis=0)
        u = lax.dynamic_slice_in_dim(w_up[0], start, quarter, axis=0)
        return dot(block, g), dot(block, u)

    a, b = received[:half], received[half:]
    r_a, l_b = to_right(a), to_left(b)
    gate, up = k_part((a, b), 0)
    a_later, b_later, gate, up, *downs = lax.optimization_barrier((a, b, gate, up, *downs))
    r_b, l_a = to_right(b_later), to_left(a_later)
    across = (to_right(r_a), to_left(l_b))
    for halves, d in (((r_a, r_b), 3), ((l_a, l_b), 1), (across, 2)):
        g, u = k_part(halves, d)
        gate, up = gate + g, up + u
    hidden = (jax.nn.silu(gate) * up).astype(BF)
    a, b = hidden[:half], hidden[half:]
    r_a, l_b = to_right(a), to_left(b)
    out = dot(hidden, lax.dynamic_slice_in_dim(w_down[0], s * quarter, quarter, axis=1))
    a_later, b_later, _ = lax.optimization_barrier((a, b, out))
    r_b, l_a = to_right(b_later), to_left(a_later)
    across = jnp.concatenate([to_right(r_a), to_left(l_b)], axis=0)
    out = out + dot(jnp.concatenate([r_a, r_b], axis=0), downs[0])
    out = out + dot(jnp.concatenate([l_a, l_b], axis=0), downs[2])
    out = out + dot(across, downs[1])
    returned = exchange(out.astype(BF))
    both = lax.dot_general(
        spread, returned, (((0,), (0,)), ((), ())), preferred_element_type=F32
    )
    return (both[:toks] + both[toks:]).astype(BF)


def solution(mesh):
    placed = (
        P(ED, None),
        P(ED, None),
        P(ED, None),
        P(ED, None, "section"),
        P(ED, None, "section"),
        P(ED, "section", None),
    )
    return jax.shard_map(
        on_device,
        mesh=mesh,
        in_specs=placed,
        out_specs=P(ED, "section"),
        check_vma=False,
    )
```

```python
import jax
import jax.numpy as jnp
from jax import lax
from jax.experimental import pallas as pl
from jax.experimental.pallas import tpu as pltpu
from jax.sharding import PartitionSpec as P

ED = ("expert", "dp")
BF = jnp.bfloat16
F32 = jnp.float32
ANY = pl.BlockSpec(memory_space=pl.ANY)
PARAMS = pltpu.CompilerParams(vmem_limit_bytes=56 * 1024 * 1024)


def dot(a, b):
    return jnp.dot(a, b, preferred_element_type=F32)


def cost(flops, read):
    return pl.CostEstimate(flops=flops, bytes_accessed=read, transcendentals=0)


def first(section, tokens, routing, gate_weights, w_down, cap, experts, sections):
    toks, fanout = routing.shape
    slots = experts * cap
    _, hid, width = w_down.shape
    quarter = width // sections
    count = sections - 1

    parts = 2
    piece = hid // parts

    def kernel(s_ref, routing_hbm, weights_hbm, tokens_hbm, down_hbm, *refs):
        rows_hbm, spread_hbm = refs[:2]
        cuts = refs[2 : 2 + count]
        (bufs, routing_ref, weights_ref, tokens_ref, rows_ref, spread_ref) = refs[2 + count : -3]
        in_sem, out_sem, small_sem = refs[-3:]

        def columns(d):
            start = lax.rem(s_ref[0] + d, sections) * quarter
            return pl.ds(pl.multiple_of(start, 128), quarter)

        small = [
            pltpu.make_async_copy(routing_hbm, routing_ref, small_sem.at[0]),
            pltpu.make_async_copy(weights_hbm, weights_ref, small_sem.at[1]),
            pltpu.make_async_copy(tokens_hbm.at[:, columns(0)], tokens_ref, small_sem.at[2]),
        ]
        ins, outs = [], []
        for d in range(count):
            for p in range(parts):
                n = d * parts + p
                at = pl.ds(p * piece, piece)
                ins.append(
                    pltpu.make_async_copy(
                        down_hbm.at[0, at, columns(d + 1)], bufs.at[n], in_sem.at[n]
                    )
                )
                outs.append(pltpu.make_async_copy(bufs.at[n], cuts[d].at[at, :], out_sem.at[n]))
        for c in small + ins:
            c.start()
        for c in small:
            c.wait()
        slot = lax.broadcasted_iota(jnp.int32, (slots, toks), 0)
        expert, order = lax.div(slot, cap), lax.rem(slot, cap)
        named = jnp.zeros((slots, toks), F32)
        weight = jnp.zeros((slots, toks), F32)
        for k in range(fanout):
            hit = routing_ref[k : k + 1, :] == expert
            named = jnp.where(hit, 1.0, named)
            weight = jnp.where(hit, weights_ref[k : k + 1, :], weight)
        before = (
            lax.broadcasted_iota(jnp.int32, (toks, toks), 0)
            < lax.broadcasted_iota(jnp.int32, (toks, toks), 1)
        )
        earlier = dot(named.astype(BF), jnp.where(before, 1.0, 0.0).astype(BF))
        place = jnp.where(earlier == order.astype(F32), named, 0.0)
        rows_ref[...] = dot(place.astype(BF), tokens_ref[...]).astype(BF)
        rows_out = pltpu.make_async_copy(rows_ref, rows_hbm, small_sem.at[3])
        rows_out.start()
        for c_in, c_out in zip(ins, outs):
            c_in.wait()
            c_out.start()
        spread = place * weight
        high = spread.astype(BF)
        spread_ref[...] = jnp.concatenate([high, (spread - high.astype(F32)).astype(BF)], axis=1)
        spread_out = pltpu.make_async_copy(spread_ref, spread_hbm, small_sem.at[4])
        spread_out.start()
        for c in outs + [rows_out, spread_out]:
            c.wait()

    rows, spread, *cut = pl.pallas_call(
        kernel,
        in_specs=[pl.BlockSpec(memory_space=pltpu.SMEM)] + [ANY] * 4,
        out_specs=[ANY] * (2 + count),
        out_shape=[
            jax.ShapeDtypeStruct((slots, quarter), BF),
            jax.ShapeDtypeStruct((slots, 2 * toks), BF),
        ]
        + [jax.ShapeDtypeStruct((hid, quarter), BF)] * count,
        scratch_shapes=[
            pltpu.VMEM((count * parts, piece, quarter), BF),
            pltpu.VMEM((fanout, toks), jnp.int32),
            pltpu.VMEM((fanout, toks), F32),
            pltpu.VMEM((toks, quarter), BF),
            pltpu.VMEM((slots, quarter), BF),
            pltpu.VMEM((slots, 2 * toks), BF),
            pltpu.SemaphoreType.DMA((count * parts,)),
            pltpu.SemaphoreType.DMA((count * parts,)),
            pltpu.SemaphoreType.DMA((5,)),
        ],
        compiler_params=PARAMS,
        cost_estimate=cost(
            2 * slots * toks * quarter, 2 * slots * quarter + 4 * count * hid * quarter
        ),
        name="first",
    )(section, routing.T, gate_weights.T, tokens, w_down)
    return rows, spread, cut


def on_device(tokens, routing, gate_weights, w_gate, w_up, w_down):
    toks, width = tokens.shape
    fanout = routing.shape[1]
    experts = lax.axis_size(ED)
    sections = lax.axis_size("section")
    cap = min(toks, max(2, 2 * toks * fanout // experts))
    quarter = width // sections
    s = lax.axis_index("section").astype(jnp.int32)

    def send(v, d):
        return lax.ppermute(v, "section", [(k, (k + d) % sections) for k in range(sections)])

    def to_right(v):
        return send(v, 1)

    def to_left(v):
        return send(v, sections - 1)

    def exchange(v):
        rows, w = v.shape
        return lax.all_to_all(
            v.reshape(experts, cap, w), ED, split_axis=0, concat_axis=0, tiled=True
        ).reshape(rows, w)

    outgoing, spread, cut = first(
        s.reshape(1), tokens, routing, gate_weights, w_down, cap, experts, sections
    )
    downs = [send(c, d + 1) for d, c in enumerate(cut)]
    received = exchange(outgoing)
    rows = experts * cap
    half = rows // 2

    def k_part(halves, d):
        block = jnp.concatenate(halves, axis=0)
        start = lax.rem(s + d, sections) * quarter
        g = lax.dynamic_slice_in_dim(w_gate[0], start, quarter, axis=0)
        u = lax.dynamic_slice_in_dim(w_up[0], start, quarter, axis=0)
        return dot(block, g), dot(block, u)

    a, b = received[:half], received[half:]
    r_a, l_b = to_right(a), to_left(b)
    gate, up = k_part((a, b), 0)
    a_later, b_later, gate, up, *downs = lax.optimization_barrier((a, b, gate, up, *downs))
    r_b, l_a = to_right(b_later), to_left(a_later)
    across = (to_right(r_a), to_left(l_b))
    for halves, d in (((r_a, r_b), 3), ((l_a, l_b), 1), (across, 2)):
        g, u = k_part(halves, d)
        gate, up = gate + g, up + u
    hidden = (jax.nn.silu(gate) * up).astype(BF)
    a, b = hidden[:half], hidden[half:]
    r_a, l_b = to_right(a), to_left(b)
    out = dot(hidden, lax.dynamic_slice_in_dim(w_down[0], s * quarter, quarter, axis=1))
    a_later, b_later, _ = lax.optimization_barrier((a, b, out))
    r_b, l_a = to_right(b_later), to_left(a_later)
    across = jnp.concatenate([to_right(r_a), to_left(l_b)], axis=0)
    out = out + dot(jnp.concatenate([r_a, r_b], axis=0), downs[0])
    out = out + dot(jnp.concatenate([l_a, l_b], axis=0), downs[2])
    out = out + dot(across, downs[1])
    returned = exchange(out.astype(BF))
    both = lax.dot_general(
        spread, returned, (((0,), (0,)), ((), ())), preferred_element_type=F32
    )
    return (both[:toks] + both[toks:]).astype(BF)


def solution(mesh):
    placed = (
        P(ED, None),
        P(ED, None),
        P(ED, None),
        P(ED, None, "section"),
        P(ED, None, "section"),
        P(ED, "section", None),
    )
    return jax.shard_map(
        on_device,
        mesh=mesh,
        in_specs=placed,
        out_specs=P(ED, "section"),
        check_vma=False,
    )
```

```python
import jax
import jax.numpy as jnp
from jax import lax
from jax.experimental import pallas as pl
from jax.experimental.pallas import tpu as pltpu
from jax.sharding import PartitionSpec as P

ED = ("expert", "dp")
BF = jnp.bfloat16
F32 = jnp.float32
ANY = pl.BlockSpec(memory_space=pl.ANY)
PARAMS = pltpu.CompilerParams(vmem_limit_bytes=56 * 1024 * 1024)


def dot(a, b):
    return jnp.dot(a, b, preferred_element_type=F32)


def cost(flops, read):
    return pl.CostEstimate(flops=flops, bytes_accessed=read, transcendentals=0)


def first(section, tokens, routing, gate_weights, w_down, cap, experts, sections):
    toks, fanout = routing.shape
    slots = experts * cap
    _, hid, width = w_down.shape
    quarter = width // sections
    count = sections - 1

    parts = 2
    piece = hid // parts

    def kernel(s_ref, routing_hbm, weights_hbm, tokens_hbm, down_hbm, *refs):
        rows_hbm, spread_hbm = refs[:2]
        cuts = refs[2 : 2 + count]
        (bufs, routing_ref, weights_ref, tokens_ref, rows_ref, spread_ref) = refs[2 + count : -3]
        in_sem, out_sem, small_sem = refs[-3:]

        def columns(d):
            start = lax.rem(s_ref[0] + d, sections) * quarter
            return pl.ds(pl.multiple_of(start, 128), quarter)

        small = [
            pltpu.make_async_copy(routing_hbm, routing_ref, small_sem.at[0]),
            pltpu.make_async_copy(weights_hbm, weights_ref, small_sem.at[1]),
            pltpu.make_async_copy(tokens_hbm.at[:, columns(0)], tokens_ref, small_sem.at[2]),
        ]
        ins, outs = [], []
        for d in range(count):
            for p in range(parts):
                n = d * parts + p
                at = pl.ds(p * piece, piece)
                ins.append(
                    pltpu.make_async_copy(
                        down_hbm.at[0, at, columns(d + 1)], bufs.at[n], in_sem.at[n]
                    )
                )
                outs.append(pltpu.make_async_copy(bufs.at[n], cuts[d].at[at, :], out_sem.at[n]))
        for c in small + ins:
            c.start()
        for c in small:
            c.wait()
        slot = lax.broadcasted_iota(jnp.int32, (slots, toks), 0)
        expert, order = lax.div(slot, cap), lax.rem(slot, cap)
        named = jnp.zeros((slots, toks), F32)
        weight = jnp.zeros((slots, toks), F32)
        for k in range(fanout):
            hit = routing_ref[k : k + 1, :] == expert
            named = jnp.where(hit, 1.0, named)
            weight = jnp.where(hit, weights_ref[k : k + 1, :], weight)
        before = (
            lax.broadcasted_iota(jnp.int32, (toks, toks), 0)
            < lax.broadcasted_iota(jnp.int32, (toks, toks), 1)
        )
        earlier = dot(named.astype(BF), jnp.where(before, 1.0, 0.0).astype(BF))
        place = jnp.where(earlier == order.astype(F32), named, 0.0)
        rows_ref[...] = dot(place.astype(BF), tokens_ref[...]).astype(BF)
        rows_out = pltpu.make_async_copy(rows_ref, rows_hbm, small_sem.at[3])
        rows_out.start()
        for c_in, c_out in zip(ins, outs):
            c_in.wait()
            c_out.start()
        spread = place * weight
        high = spread.astype(BF)
        spread_ref[...] = jnp.concatenate([high, (spread - high.astype(F32)).astype(BF)], axis=1)
        spread_out = pltpu.make_async_copy(spread_ref, spread_hbm, small_sem.at[4])
        spread_out.start()
        for c in outs + [rows_out, spread_out]:
            c.wait()

    rows, spread, *cut = pl.pallas_call(
        kernel,
        in_specs=[pl.BlockSpec(memory_space=pltpu.SMEM)] + [ANY] * 4,
        out_specs=[ANY] * (2 + count),
        out_shape=[
            jax.ShapeDtypeStruct((slots, quarter), BF),
            jax.ShapeDtypeStruct((slots, 2 * toks), BF),
        ]
        + [jax.ShapeDtypeStruct((hid, quarter), BF)] * count,
        scratch_shapes=[
            pltpu.VMEM((count * parts, piece, quarter), BF),
            pltpu.VMEM((fanout, toks), jnp.int32),
            pltpu.VMEM((fanout, toks), F32),
            pltpu.VMEM((toks, quarter), BF),
            pltpu.VMEM((slots, quarter), BF),
            pltpu.VMEM((slots, 2 * toks), BF),
            pltpu.SemaphoreType.DMA((count * parts,)),
            pltpu.SemaphoreType.DMA((count * parts,)),
            pltpu.SemaphoreType.DMA((5,)),
        ],
        compiler_params=PARAMS,
        cost_estimate=cost(
            2 * slots * toks * quarter, 2 * slots * quarter + 4 * count * hid * quarter
        ),
        name="first",
    )(section, routing.T, gate_weights.T, tokens, w_down)
    return rows, spread, cut


def on_device(tokens, routing, gate_weights, w_gate, w_up, w_down):
    toks, width = tokens.shape
    fanout = routing.shape[1]
    experts = lax.axis_size(ED)
    sections = lax.axis_size("section")
    cap = min(toks, max(2, 2 * toks * fanout // experts))
    quarter = width // sections
    s = lax.axis_index("section").astype(jnp.int32)

    def send(v, d):
        return lax.ppermute(v, "section", [(k, (k + d) % sections) for k in range(sections)])

    def to_right(v):
        return send(v, 1)

    def to_left(v):
        return send(v, sections - 1)

    def exchange(v):
        rows, w = v.shape
        return lax.all_to_all(
            v.reshape(experts, cap, w), ED, split_axis=0, concat_axis=0, tiled=True
        ).reshape(rows, w)

    outgoing, spread, cut = first(
        s.reshape(1), tokens, routing, gate_weights, w_down, cap, experts, sections
    )
    downs = [send(c, d + 1) for d, c in enumerate(cut)]
    received = exchange(outgoing)
    rows = experts * cap
    half = rows // 2

    def k_part(halves, d):
        block = jnp.concatenate(halves, axis=0)
        start = lax.rem(s + d, sections) * quarter
        g = lax.dynamic_slice_in_dim(w_gate[0], start, quarter, axis=0)
        u = lax.dynamic_slice_in_dim(w_up[0], start, quarter, axis=0)
        return dot(block, g), dot(block, u)

    a, b = received[:half], received[half:]
    r_a, l_b = to_right(a), to_left(b)
    gate, up = k_part((a, b), 0)
    a_later, b_later, gate, up, *downs = lax.optimization_barrier((a, b, gate, up, *downs))
    r_b, l_a = to_right(b_later), to_left(a_later)
    across = (to_right(r_a), to_left(l_b))
    for halves, d in (((r_a, r_b), 3), ((l_a, l_b), 1), (across, 2)):
        g, u = k_part(halves, d)
        gate, up = gate + g, up + u
    hidden = (jax.nn.silu(gate) * up).astype(BF)
    a, b = hidden[:half], hidden[half:]
    r_a, l_b = to_right(a), to_left(b)
    out = dot(hidden, lax.dynamic_slice_in_dim(w_down[0], s * quarter, quarter, axis=1))
    a_later, b_later, _ = lax.optimization_barrier((a, b, out))
    r_b, l_a = to_right(b_later), to_left(a_later)
    across = jnp.concatenate([to_right(r_a), to_left(l_b)], axis=0)
    near = jnp.concatenate(
        [jnp.concatenate([r_a, r_b], axis=0), jnp.concatenate([l_a, l_b], axis=0)], axis=1
    )
    out = out + dot(near, jnp.concatenate([downs[0], downs[2]], axis=0))
    out = out + dot(across, downs[1])
    returned = exchange(out.astype(BF))
    both = lax.dot_general(
        spread, returned, (((0,), (0,)), ((), ())), preferred_element_type=F32
    )
    return (both[:toks] + both[toks:]).astype(BF)


def solution(mesh):
    placed = (
        P(ED, None),
        P(ED, None),
        P(ED, None),
        P(ED, None, "section"),
        P(ED, None, "section"),
        P(ED, "section", None),
    )
    return jax.shard_map(
        on_device,
        mesh=mesh,
        in_specs=placed,
        out_specs=P(ED, "section"),
        check_vma=False,
    )
```

```python
import jax
import jax.numpy as jnp
from jax import lax
from jax.experimental import pallas as pl
from jax.experimental.pallas import tpu as pltpu
from jax.sharding import PartitionSpec as P

ED = ("expert", "dp")
BF = jnp.bfloat16
F32 = jnp.float32
ANY = pl.BlockSpec(memory_space=pl.ANY)
PARAMS = pltpu.CompilerParams(vmem_limit_bytes=56 * 1024 * 1024)


def dot(a, b):
    return jnp.dot(a, b, preferred_element_type=F32)


def cost(flops, read):
    return pl.CostEstimate(flops=flops, bytes_accessed=read, transcendentals=0)


def first(section, tokens, routing, gate_weights, w_down, cap, experts, sections):
    toks, fanout = routing.shape
    slots = experts * cap
    _, hid, width = w_down.shape
    quarter = width // sections
    count = sections - 1

    parts = 2
    piece = hid // parts

    def kernel(s_ref, routing_hbm, weights_hbm, tokens_hbm, down_hbm, *refs):
        rows_hbm, spread_hbm = refs[:2]
        cuts = refs[2 : 2 + count]
        (bufs, routing_ref, weights_ref, tokens_ref, rows_ref, spread_ref) = refs[2 + count : -3]
        in_sem, out_sem, small_sem = refs[-3:]

        def columns(d):
            start = lax.rem(s_ref[0] + d, sections) * quarter
            return pl.ds(pl.multiple_of(start, 128), quarter)

        small = [
            pltpu.make_async_copy(routing_hbm, routing_ref, small_sem.at[0]),
            pltpu.make_async_copy(weights_hbm, weights_ref, small_sem.at[1]),
            pltpu.make_async_copy(tokens_hbm.at[:, columns(0)], tokens_ref, small_sem.at[2]),
        ]
        ins, outs = [], []
        for d in range(count):
            for p in range(parts):
                n = d * parts + p
                at = pl.ds(p * piece, piece)
                ins.append(
                    pltpu.make_async_copy(
                        down_hbm.at[0, at, columns(d + 1)], bufs.at[n], in_sem.at[n]
                    )
                )
                outs.append(pltpu.make_async_copy(bufs.at[n], cuts[d].at[at, :], out_sem.at[n]))
        for c in small + ins:
            c.start()
        for c in small:
            c.wait()
        slot = lax.broadcasted_iota(jnp.int32, (slots, toks), 0)
        expert, order = lax.div(slot, cap), lax.rem(slot, cap)
        named = jnp.zeros((slots, toks), F32)
        weight = jnp.zeros((slots, toks), F32)
        for k in range(fanout):
            hit = routing_ref[k : k + 1, :] == expert
            named = jnp.where(hit, 1.0, named)
            weight = jnp.where(hit, weights_ref[k : k + 1, :], weight)
        before = (
            lax.broadcasted_iota(jnp.int32, (toks, toks), 0)
            < lax.broadcasted_iota(jnp.int32, (toks, toks), 1)
        )
        earlier = dot(named.astype(BF), jnp.where(before, 1.0, 0.0).astype(BF))
        place = jnp.where(earlier == order.astype(F32), named, 0.0)
        rows_ref[...] = dot(place.astype(BF), tokens_ref[...]).astype(BF)
        rows_out = pltpu.make_async_copy(rows_ref, rows_hbm, small_sem.at[3])
        rows_out.start()
        for c_in, c_out in zip(ins, outs):
            c_in.wait()
            c_out.start()
        spread = place * weight
        high = spread.astype(BF)
        spread_ref[...] = jnp.concatenate([high, (spread - high.astype(F32)).astype(BF)], axis=1)
        spread_out = pltpu.make_async_copy(spread_ref, spread_hbm, small_sem.at[4])
        spread_out.start()
        for c in outs + [rows_out, spread_out]:
            c.wait()

    rows, spread, *cut = pl.pallas_call(
        kernel,
        in_specs=[pl.BlockSpec(memory_space=pltpu.SMEM)] + [ANY] * 4,
        out_specs=[ANY] * (2 + count),
        out_shape=[
            jax.ShapeDtypeStruct((slots, quarter), BF),
            jax.ShapeDtypeStruct((slots, 2 * toks), BF),
        ]
        + [jax.ShapeDtypeStruct((hid, quarter), BF)] * count,
        scratch_shapes=[
            pltpu.VMEM((count * parts, piece, quarter), BF),
            pltpu.VMEM((fanout, toks), jnp.int32),
            pltpu.VMEM((fanout, toks), F32),
            pltpu.VMEM((toks, quarter), BF),
            pltpu.VMEM((slots, quarter), BF),
            pltpu.VMEM((slots, 2 * toks), BF),
            pltpu.SemaphoreType.DMA((count * parts,)),
            pltpu.SemaphoreType.DMA((count * parts,)),
            pltpu.SemaphoreType.DMA((5,)),
        ],
        compiler_params=PARAMS,
        cost_estimate=cost(
            2 * slots * toks * quarter, 2 * slots * quarter + 4 * count * hid * quarter
        ),
        name="first",
    )(section, routing.T, gate_weights.T, tokens, w_down)
    return rows, spread, cut


def on_device(tokens, routing, gate_weights, w_gate, w_up, w_down):
    toks, width = tokens.shape
    fanout = routing.shape[1]
    experts = lax.axis_size(ED)
    sections = lax.axis_size("section")
    cap = min(toks, max(2, 2 * toks * fanout // experts))
    quarter = width // sections
    s = lax.axis_index("section").astype(jnp.int32)

    def send(v, d):
        return lax.ppermute(v, "section", [(k, (k + d) % sections) for k in range(sections)])

    def to_right(v):
        return send(v, 1)

    def to_left(v):
        return send(v, sections - 1)

    def exchange(v):
        rows, w = v.shape
        return lax.all_to_all(
            v.reshape(experts, cap, w), ED, split_axis=0, concat_axis=0, tiled=True
        ).reshape(rows, w)

    outgoing, spread, cut = first(
        s.reshape(1), tokens, routing, gate_weights, w_down, cap, experts, sections
    )
    downs = [send(c, d + 1) for d, c in enumerate(cut)]
    received = exchange(outgoing)
    rows = experts * cap
    half = rows // 2

    def k_part(halves, d):
        block = jnp.concatenate(halves, axis=0)
        start = lax.rem(s + d, sections) * quarter
        g = lax.dynamic_slice_in_dim(w_gate[0], start, quarter, axis=0)
        u = lax.dynamic_slice_in_dim(w_up[0], start, quarter, axis=0)
        return dot(block, g), dot(block, u)

    a, b = received[:half], received[half:]
    r_a, l_b = to_right(a), to_left(b)
    gate, up = k_part((a, b), 0)
    a_later, b_later, gate, up, *downs = lax.optimization_barrier((a, b, gate, up, *downs))
    r_b, l_a = to_right(b_later), to_left(a_later)
    across = (to_right(r_a), to_left(l_b))
    for halves, d in (((r_a, r_b), 3), ((l_a, l_b), 1), (across, 2)):
        g, u = k_part(halves, d)
        gate, up = gate + g, up + u
    hidden = (jax.nn.silu(gate) * up).astype(BF)
    a, b = hidden[:half], hidden[half:]
    r_a, l_b = to_right(a), to_left(b)
    out = dot(hidden, lax.dynamic_slice_in_dim(w_down[0], s * quarter, quarter, axis=1))
    a_later, b_later, _ = lax.optimization_barrier((a, b, out))
    r_b, l_a = to_right(b_later), to_left(a_later)
    across = jnp.concatenate([to_right(r_a), to_left(l_b)], axis=0)
    near = jnp.concatenate(
        [jnp.concatenate([r_a, r_b], axis=0), jnp.concatenate([l_a, l_b], axis=0)], axis=1
    )
    out = out + dot(near, jnp.concatenate([downs[0], downs[2]], axis=0))
    out = lax.optimization_barrier(out) + dot(across, downs[1])
    returned = exchange(out.astype(BF))
    both = lax.dot_general(
        spread, returned, (((0,), (0,)), ((), ())), preferred_element_type=F32
    )
    return (both[:toks] + both[toks:]).astype(BF)


def solution(mesh):
    placed = (
        P(ED, None),
        P(ED, None),
        P(ED, None),
        P(ED, None, "section"),
        P(ED, None, "section"),
        P(ED, "section", None),
    )
    return jax.shard_map(
        on_device,
        mesh=mesh,
        in_specs=placed,
        out_specs=P(ED, "section"),
        check_vma=False,
    )
```
